32 devices in a mesh: row: 4 (over y, x), col: 8 (over z, core).
Axes of the slice: x: 2, y: 2, z: 4, core: 2. Of those that a mesh axis runs over, the one named last changes fastest.
Arguments:
- residual_in: float32 [8, 4, 32, 256], P(None, 'row', None, 'col'), may hold values from -6 to 6
- diag_inverse: bfloat16 [8, 4, 256, 256], P(None, 'row'), may hold values from -0.04 to 1.04, as said below
- lower_blocks: bfloat16 [7, 4, 3, 256, 256], P(None, 'row'), may hold values from -0.15625 to 0.15625
- column_lists: int32 [7, 4, 3], replicated, may hold values from 0 to 27, as said below
Outputs:
- precond: float32 [8, 4, 32, 256], P(None, 'row', None, 'col')
The draws below stay inside these ranges and needn't reach their ends.
Inputs may be any that keep to these rules, and one draw needn't show every extreme that they name: `column_lists`: for a block row of level s, every entry names a block row of a level below s; its first entry names a block row of level s - 1, and every block row of level s - 1 is named so by exactly one block row of level s. `diag_inverse`: each block is the identity plus small entries.
All inputs are finite; a program needn't handle non-finite values.
Results may differ from the reference program's by a relative error of at most 0.0003.
Values sent between devices are 32-bit elements; how exact they have to be, the bound alone decides.
No kernel may reach another device: no remote copies, remote signals or barrier semaphores. Data moves between devices by JAX's collectives and lax.ppermute only.
A program may use at most 64 MiB of HBM per device.

```python
import jax
import jax.numpy as jnp
from jax import lax

BS = 256
KB = 3
SLOTS = 8
OWNERS = 4
PROBES = 32


def draw_column_lists(key, part):
    shifts = jax.random.randint(jax.random.fold_in(key, 11), (SLOTS - 1, 1), 0, OWNERS)
    owner_ids = jnp.arange(OWNERS, dtype=jnp.int32)[None, :]
    levels = jnp.arange(1, SLOTS, dtype=jnp.int32)[:, None]
    leading = (levels - 1) * OWNERS + (owner_ids + shifts) % OWNERS
    limits = jnp.broadcast_to((levels * OWNERS)[:, :, None], (SLOTS - 1, OWNERS, KB - 1))
    others = jax.random.randint(jax.random.fold_in(key, 12), (SLOTS - 1, OWNERS, KB - 1), 0, limits)
    return jnp.concatenate([leading[:, :, None], others], axis=2).astype(jnp.int32)


def draw_diag_inverse(key, part):
    identity = (jnp.arange(BS)[:, None] == jnp.arange(BS)[None, :]).astype(jnp.float32)
    shape = (SLOTS, OWNERS, BS, BS)
    noise = jax.random.uniform(key, shape, jnp.float32, -0.03, 0.03)
    return (identity + noise).astype(jnp.bfloat16)


def shard_levels(key, dims, pieces, least, largest):
    loudness = 1.0
    for dim, shards_of in pieces:
        heights = jax.random.uniform(jax.random.fold_in(jax.random.fold_in(key, 6), dim), (shards_of,), jnp.float32, least / len(pieces), largest / len(pieces))
        loudness = loudness * jnp.repeat(jnp.exp(heights), dims[dim] // shards_of).reshape((-1,) + (1,) * (len(dims) - 1 - dim))
    return loudness


def scatter_about(own_key, dims, spread, limit, cuts=(), kind=jnp.bfloat16):
    result = jax.random.normal(own_key, dims, jnp.float32) * spread
    if len(cuts) > 0:
        result = shard_levels(own_key, dims, cuts, -0.22, 0.18) * result
    return jnp.clip(result, min=-limit, max=limit).astype(kind)


def setup_inputs(seed: int = 0) -> dict:
    keys = jax.random.split(jax.random.key(seed), 5)
    return {
        "residual_in": scatter_about(keys[0], (SLOTS, OWNERS, PROBES, BS), 1.0, 6.0, ((1, 4), (3, 8)), jnp.float32),
        "diag_inverse": draw_diag_inverse(jax.random.fold_in(keys[4], 71), 0),
        "lower_blocks": scatter_about(keys[2], (SLOTS - 1, OWNERS, KB, BS, BS), (6 * BS) ** -0.5, 0.15625, ((1, 4),)),
        "column_lists": draw_column_lists(jax.random.fold_in(keys[4], 71), 0),
    }


def reference(residual_in, diag_inverse, lower_blocks, column_lists):
    highest = lax.Precision.HIGHEST
    inverses = diag_inverse.astype(jnp.float32)
    lowers = lower_blocks.astype(jnp.float32)
    total_blocks = SLOTS * OWNERS
    forward = jnp.zeros((total_blocks, PROBES, BS), jnp.float32)
    for current in range(SLOTS):
        source = residual_in[current]
        if current > 0:
            pulled = forward[column_lists[current - 1]]
            source = source - jnp.einsum("rkpc,rkdc->rpd", pulled, lowers[current - 1], precision=highest)
        solved = jnp.einsum("rpc,rdc->rpd", source, inverses[current], precision=highest)
        forward = forward.at[current * OWNERS:(current + 1) * OWNERS].set(solved)
    accumulated = jnp.zeros((total_blocks, PROBES, BS), jnp.float32)
    backward = jnp.zeros((total_blocks, PROBES, BS), jnp.float32)
    for current in reversed(range(SLOTS)):
        lower_end = current * OWNERS
        upper_end = (current + 1) * OWNERS
        source = forward[lower_end:upper_end] - accumulated[lower_end:upper_end]
        solved = jnp.einsum("rpc,rcd->rpd", source, inverses[current], precision=highest)
        backward = backward.at[lower_end:upper_end].set(solved)
        if current > 0:
            contributions = jnp.einsum("rpd,rkdc->rkpc", solved, lowers[current - 1], precision=highest)
            targets = column_lists[current - 1].reshape(-1).astype(jnp.int32)
            accumulated = accumulated.at[targets].add(contributions.reshape(-1, PROBES, BS))
    return backward.reshape(SLOTS, OWNERS, PROBES, BS)
```

```python
import functools

import jax
import jax.numpy as jnp
from jax import lax
from jax.experimental import pallas as pl
from jax.experimental.pallas import tpu as pltpu
from jax.sharding import PartitionSpec as P

VMEM = pltpu.VMEM
SMEM = pltpu.SMEM


def two_parts(rows):
    high = rows.astype(jnp.bfloat16).astype(jnp.float32)
    return jnp.concatenate([high, rows - high], axis=0).astype(jnp.bfloat16)


def times(rows, block, transposed):
    contract = 1 if transposed else 0
    product = lax.dot_general(
        two_parts(rows), block, (((1,), (contract,)), ((), ())),
        preferred_element_type=jnp.float32,
    )
    count = rows.shape[0]
    return product[:count] + product[count:]


def first_kernel(owners, lists, me, source, inverses, finished, solved):
    answer = times(source[0], inverses[0], True)
    finished[me[0]] = answer
    solved[...] = answer


def forward_kernel(level, owners, blocks, lists, me, source, inverses, lowers, finished_in, *rest):
    arrived, (finished, solved) = rest[: owners - 1], rest[owners - 1 :]
    own = me[0]
    for mask in range(1, owners):
        finished[(level - 1) * owners + (own ^ mask)] = arrived[mask - 1][...]
    total = source[level]
    for k in range(blocks):
        pulled = finished[lists[((level - 1) * owners + own) * blocks + k]]
        total = total - times(pulled, lowers[level - 1, k], True)
    answer = times(total, inverses[level], True)
    finished[level * owners + own] = answer
    solved[...] = answer


def backward_kernel(level, levels, owners, blocks, lists, me, inverses, lowers, finished, *rest):
    own = me[0]
    top = level == levels - 1
    rest = list(rest)
    if top:
        (accumulated, answers, sent) = rest
        accumulated[...] = jnp.zeros_like(accumulated)
        answers[...] = jnp.zeros_like(answers)
    else:
        arrived, rest = rest[: owners - 1], rest[owners - 1 :]
        (_, _, accumulated, answers, *sent) = rest
        for mask in range(1, owners):
            for k in range(blocks):
                column = lists[(level * owners + (own ^ mask)) * blocks + k]
                mine = (lax.rem(column, owners) == own).astype(jnp.float32)
                slot = lax.div(column, owners)
                accumulated[slot] += mine * arrived[mask - 1][k]
        sent = sent[0] if sent else None
    source = finished[level * owners + own] - accumulated[level]
    answer = times(source, inverses[level], False)
    answers[level] = answer
    if level > 0:
        for k in range(blocks):
            product = times(answer, lowers[level - 1, k], False)
            sent[k] = product
            column = lists[((level - 1) * owners + own) * blocks + k]
            mine = (lax.rem(column, owners) == own).astype(jnp.float32)
            slot = lax.div(column, owners)
            accumulated[slot] += mine * product


def in_vmem(array):
    return pltpu.with_memory_space_constraint(array, VMEM)


def shards(residual_in, diag_inverse, lower_blocks, column_lists):
    sweep_input = lax.all_to_all(residual_in, "col", split_axis=2, concat_axis=3, tiled=True)[:, 0]
    levels, probes, size = sweep_input.shape
    owners = lax.axis_size("row")
    blocks = column_lists.shape[2]
    me = lax.axis_index("row").astype(jnp.int32).reshape(1)
    lists = column_lists.reshape(-1)
    inverses = in_vmem(diag_inverse[:, 0])
    lowers = in_vmem(lower_blocks[:, 0])
    sweep_input = in_vmem(sweep_input)
    vmem = pl.BlockSpec(memory_space=VMEM)
    smem = pl.BlockSpec(memory_space=SMEM)
    params = pltpu.CompilerParams(vmem_limit_bytes=16 * 2**20)
    rows = VMEM((probes, size), jnp.float32)
    all_rows = VMEM((levels * owners, probes, size), jnp.float32)
    own_rows = VMEM((levels, probes, size), jnp.float32)
    products = VMEM((blocks, probes, size), jnp.float32)

    def exchange(array):
        return [
            in_vmem(lax.ppermute(array, "row", [(i, i ^ mask) for i in range(owners)]))
            for mask in range(1, owners)
        ]

    finished, solved = pl.pallas_call(
        functools.partial(first_kernel, owners),
        in_specs=[smem, smem, vmem, vmem],
        out_specs=[vmem, vmem],
        out_shape=[all_rows, rows],
        compiler_params=params,
        name="forward_first",
    )(lists, me, sweep_input, inverses)
    for level in range(1, levels):
        arrived = exchange(solved)
        finished, solved = pl.pallas_call(
            functools.partial(forward_kernel, level, owners, blocks),
            in_specs=[smem, smem] + [vmem] * (4 + owners - 1),
            out_specs=[vmem, vmem],
            out_shape=[all_rows, rows],
            input_output_aliases={5: 0},
            compiler_params=params,
            name="forward_level",
        )(lists, me, sweep_input, inverses, lowers, in_vmem(finished), *arrived)

    finished = in_vmem(finished)
    accumulated, answers, sent = pl.pallas_call(
        functools.partial(backward_kernel, levels - 1, levels, owners, blocks),
        in_specs=[smem, smem, vmem, vmem, vmem],
        out_specs=[vmem] * 3,
        out_shape=[own_rows, own_rows, products],
        compiler_params=params,
        name="backward_first",
    )(lists, me, inverses, lowers, finished)
    for level in reversed(range(levels - 1)):
        arrived = exchange(sent)
        base = 5 + owners - 1
        out = pl.pallas_call(
            functools.partial(backward_kernel, level, levels, owners, blocks),
            in_specs=[smem, smem] + [vmem] * (3 + owners - 1 + 2),
            out_specs=[vmem] * (3 if level else 2),
            out_shape=[own_rows, own_rows] + ([products] if level else []),
            input_output_aliases={base: 0, base + 1: 1},
            compiler_params=params,
            name="backward_level",
        )(lists, me, inverses, lowers, finished, *arrived, in_vmem(accumulated), in_vmem(answers))
        accumulated, answers = out[:2]
        sent = out[2] if level else None
    return lax.all_to_all(answers[:, None], "col", split_axis=3, concat_axis=2, tiled=True)


def solution(mesh):
    placed = (
        P(None, "row", None, "col"),
        P(None, "row", None, None),
        P(None, "row", None, None, None),
        P(),
    )
    return jax.shard_map(
        shards, mesh=mesh, in_specs=placed, out_specs=P(None, "row", None, "col"), check_vma=False
    )
```

```python
import types

import jax
import jax.numpy as jnp
from jax import lax
from jax.experimental import pallas as pl
from jax.experimental.pallas import tpu as pltpu
from jax.sharding import PartitionSpec as P

VMEM = pltpu.VMEM
SMEM = pltpu.SMEM
F32 = jnp.float32
BF16 = jnp.bfloat16
GROUPS = ()
SCALARS = ("lists", "listed")
FAR = ("residual", "diag_inverse", "lower_blocks", "gathered")


def two_parts(rows):
    high = rows.astype(BF16).astype(F32)
    return jnp.concatenate([high, rows - high], axis=0).astype(BF16)


def times(rows, block, transposed):
    contract = 1 if transposed else 0
    product = lax.dot_general(
        two_parts(rows), block, (((1,), (contract,)), ((), ())), preferred_element_type=F32
    )
    count = rows.shape[0]
    return product[:count] + product[count:]


def lane_group(shape, width):
    return lax.broadcasted_iota(jnp.int32, shape, 1) // width


def regroup(pieces, width):
    rows, size = pieces[0].shape
    groups = size // width
    stacked = jnp.concatenate(pieces, axis=0)
    rolled = [stacked if d == 0 else pltpu.roll(stacked, d * width, 1) for d in range(groups)]
    group = lane_group((rows, size), width)

    def result(b):
        total = jnp.zeros((rows, size), F32)
        for a in range(len(pieces)):
            moved = rolled[(a - b) % groups][a * rows : (a + 1) * rows]
            total = jnp.where(group == a, moved, total)
        return total

    return result


def regroup_one(pieces, width, b):
    rows, size = pieces[0].shape
    groups = size // width
    group = lane_group((rows, size), width)
    total = jnp.zeros((rows, size), F32)
    for a, piece in enumerate(pieces):
        shift = (a - b) % groups
        total = jnp.where(group == a, pltpu.roll(piece, shift * width, 1) if shift else piece, total)
    return total


def placed_in(key, array):
    if key == "listed":
        return array
    space = SMEM if key in SCALARS else pltpu.HBM if key in FAR else VMEM
    return pltpu.with_memory_space_constraint(array, space)


def call(name, body, reads, updates=None, makes=None, scratch=None, cost=None):
    updates, makes, scratch = updates or {}, makes or {}, scratch or {}
    ins = {**reads, **updates}
    outs = {key: VMEM(value.shape, value.dtype) for key, value in updates.items()} | makes
    in_names, out_names, scratch_names = list(ins), list(outs), list(scratch)

    def kernel(*refs):
        space = types.SimpleNamespace()
        for key, ref in zip(in_names + out_names + scratch_names, refs, strict=True):
            setattr(space, key, ref)
        space.place = (lax.axis_index("row"), lax.axis_index("col"))
        body(space)

    def spec(key):
        if key in SCALARS:
            return pl.BlockSpec(memory_space=SMEM)
        return pl.BlockSpec(memory_space=pltpu.HBM if key in FAR else VMEM)

    results = pl.pallas_call(
        kernel,
        in_specs=[spec(key) for key in in_names],
        out_specs=[spec(key) for key in out_names],
        out_shape=[outs[key] for key in out_names],
        input_output_aliases={in_names.index(key): out_names.index(key) for key in updates},
        scratch_shapes=list(scratch.values()),
        compiler_params=pltpu.CompilerParams(vmem_limit_bytes=24 * 2**20),
        cost_estimate=cost,
        name=name,
    )(*[placed_in(key, value) for key, value in ins.items()])
    return dict(zip(out_names, results, strict=True))


def shards(residual_in, diag_inverse, lower_blocks, column_lists):
    levels, _, probes, width = residual_in.shape
    size = diag_inverse.shape[-1]
    owners, columns = lax.axis_size("row"), lax.axis_size("col")
    each = probes // columns
    blocks = column_lists.shape[2]
    pair = 2
    shared_groups = GROUPS if owners <= 4 and blocks == 3 else ()
    shared_levels = [level for group in shared_groups for level in group]
    shared_forward = [level for level in shared_levels if level == levels - 2]
    rows = VMEM((each, size), F32)
    all_rows = VMEM((levels * owners, each, size), F32)
    own_rows = VMEM((levels, each, size), F32)
    products = VMEM((blocks, each, size), F32)
    messages = VMEM((owners * columns, 2 * each, size), F32)
    ring = [position ^ (position >> 1) for position in range(owners)]

    def exchange(array):
        return {
            f"arrived_{mask}": lax.ppermute(array, "row", [(i, i ^ mask) for i in range(owners)])
            for mask in range(1, owners)
        }

    def to_all(array):
        return lax.all_to_all(array, ("row", "col"), split_axis=0, concat_axis=0, tiled=True)

    def column_of(r, level, owner, k):
        return r.lists[((level - 1) * owners + owner) * blocks + k]

    def send_body(r):
        first = pltpu.make_async_copy(r.residual, r.near, r.sems.at[0])
        second = pltpu.make_async_copy(r.diag_inverse.at[0, 0], r.inverse, r.sems.at[1])
        first.start()
        second.start()

        def widened(array, shift):
            padded = jnp.concatenate([array, jnp.zeros((probes, size - width), F32)], axis=1)
            return pltpu.roll(padded, shift, 1)

        first.wait()
        packed = widened(r.near[1, 0], 0)
        for level in range(2, levels):
            packed = packed + widened(r.near[level, 0], (level - 1) * width)
        start = widened(r.near[0, 0], r.place[1] * width)
        second.wait()
        partial = times(start, r.inverse[...], True)
        for column in range(columns):
            part = slice(column * each, (column + 1) * each)
            message = jnp.concatenate([partial[part], packed[part]], axis=0)
            for owner in range(owners):
                r.messages[owner * columns + column] = message

    def hold_body(r):
        for i in range(r.lists.shape[0]):
            r.lists[i] = r.listed[i]
        first = pltpu.make_async_copy(r.diag_inverse.at[:, 0], r.inverses, r.sems.at[0])
        second = pltpu.make_async_copy(r.lower_blocks.at[:, 0], r.lowers, r.sems.at[1])
        first.start()
        second.start()
        first.wait()
        second.wait()

    def widen_body(group):
        def body(r):
            half = lax.rem(r.place[1], pair)

            @pl.when(half == 0)
            def _():
                copies = []
                for n, level in enumerate(group):
                    copies.append(pltpu.make_async_copy(r.diag_inverse.at[level, 0], r.near.at[n, 0], r.sems.at[n, 0]))
                    copies.append(pltpu.make_async_copy(r.lower_blocks.at[level - 1, 0, 0], r.near.at[n, 1], r.sems.at[n, 1]))
                for copy in copies:
                    copy.start()
                for copy in copies:
                    copy.wait()

            @pl.when(half != 0)
            def _():
                copies = []
                for n, level in enumerate(group):
                    for k in (1, 2):
                        source = r.lower_blocks.at[level - 1, 0, k]
                        copies.append(pltpu.make_async_copy(source, r.near.at[n, k - 1], r.sems.at[n, k - 1]))
                for copy in copies:
                    copy.start()
                for copy in copies:
                    copy.wait()

            r.wide[...] = r.near[...].astype(F32)

        return body

    def narrow_body(n):
        def body(r):
            copies = [
                pltpu.make_async_copy(r.gathered.at[p, n], r.near.at[p], r.sems.at[p]) for p in range(owners * pair)
            ]
            for copy in copies:
                copy.start()
            for p, copy in enumerate(copies):
                copy.wait()
                r.shared[p] = r.near[p].astype(BF16)

        return body

    def shared_block(r, owner, k):
        return r.shared[ring.index(owner) * pair + k // 2, k % 2]

    def own_forward(r, level):
        own = r.place[0]
        total = r.source[level]
        for k in range(blocks):
            total = total - times(r.finished[column_of(r, level, own, k)], r.lowers[level - 1, k], True)
        answer = times(total, r.inverses[level], True)
        r.finished[level * owners + own] = answer
        return answer

    def all_forward(r, level):
        answers = []
        for owner in range(owners):
            pieces = [r.received[owner * columns + c, each:] for c in range(columns)]
            total = regroup_one(pieces, width, level - 1)
            for k in range(blocks):
                total = total - times(r.finished[column_of(r, level, owner, k)], shared_block(r, owner, k + 1), True)
            answers.append(times(total, shared_block(r, owner, 0), True))
        for owner in range(owners):
            r.finished[level * owners + owner] = answers[owner]

    def own_backward(r, level):
        row = level * owners + r.place[0]
        answer = times(r.finished[row] - r.accumulated[row], r.inverses[level], False)
        r.answers[level] = answer
        return answer

    def own_products(r, level, answer):
        for k in range(blocks):
            product = times(answer, r.lowers[level - 1, k], False)
            r.sent[k] = product
            r.accumulated[column_of(r, level, r.place[0], k)] += product

    def all_backward(r, level):
        answers = []
        for owner in range(owners):
            row = level * owners + owner
            answers.append(times(r.finished[row] - r.accumulated[row], shared_block(r, owner, 0), False))
        results = [
            [times(answers[owner], shared_block(r, owner, k + 1), False) for k in range(blocks)] for owner in range(owners)
        ]
        own_answer = answers[0]
        for owner in range(1, owners):
            own_answer = jnp.where(r.place[0] == owner, answers[owner], own_answer)
        r.answers[level] = own_answer
        for owner in range(owners):
            for k in range(blocks):
                r.accumulated[column_of(r, level, owner, k)] += results[owner][k]

    def take_finished(r, level):
        for mask in range(1, owners):
            r.finished[level * owners + (r.place[0] ^ mask)] = getattr(r, f"arrived_{mask}")[...]

    def take_products(r, level):
        for mask in range(1, owners):
            for k in range(blocks):
                column = column_of(r, level, r.place[0] ^ mask, k)
                r.accumulated[column] += getattr(r, f"arrived_{mask}")[k]

    def receive_body(r):
        for owner in range(owners):
            total = r.received[owner * columns, :each]
            for column in range(1, columns):
                total = total + r.received[owner * columns + column, :each]
            r.finished[owner] = total
        moved = regroup([r.received[r.place[0] * columns + c, each:] for c in range(columns)], width)
        for level in range(1, levels):
            r.source[level] = moved(level - 1)
        r.solved[...] = own_forward(r, 1)

    def last_send(r):
        answer = own_backward(r, 1)
        r.pieces[...] = jnp.zeros_like(r.pieces)
        r.pieces[r.place[0]] = r.finished[r.place[0]] - r.accumulated[r.place[0]]
        for k in range(blocks):
            r.pieces[column_of(r, 1, r.place[0], k)] -= times(answer, r.lowers[0, k], False)
        moved = regroup([r.answers[level] for level in range(1, levels)], width)
        for column in range(columns):
            packed = moved(column)
            for owner in range(owners):
                r.messages[owner * columns + column] = jnp.concatenate([r.pieces[owner], packed], axis=0)

    def last_body(r):
        sums, packed = [], []
        for column in range(columns):
            total = r.received[column, :each]
            for owner in range(1, owners):
                total = total + r.received[owner * columns + column, :each]
            sums.append(total)
            packed.append(r.received[r.place[0] * columns + column, each:])
        answer = times(jnp.concatenate(sums, axis=0), r.inverses[0], False)
        r.out[0, 0] = pltpu.roll(answer, lax.rem(size - r.place[1] * width, size), 1)[:, :width]
        packed = jnp.concatenate(packed, axis=0)
        for level in range(1, levels):
            moved = packed if level == 1 else pltpu.roll(packed, size - (level - 1) * width, 1)
            r.out[level, 0] = moved[:, :width]

    dma = pltpu.SemaphoreType.DMA
    far_blocks = {"diag_inverse": diag_inverse, "lower_blocks": lower_blocks}

    order = [
        [owner * columns + column + half for owner in ring for half in range(pair)]
        for column in range(0, columns, pair)
    ]
    gathered = {}
    for g, group in enumerate(shared_groups):
        wide = call(
            f"widen_{g}", widen_body(group), far_blocks,
            makes={"wide": jax.ShapeDtypeStruct((len(group), 2, size, size), F32)},
            scratch={"near": VMEM((len(group), 2, size, size), BF16), "sems": dma((len(group), 2))},
        )["wide"]
        arrays = lax.all_gather(wide, ("row", "col"), axis=0, axis_index_groups=order)
        for n, level in enumerate(group):
            gathered[level] = (arrays, n)

    def shared_of(level, after):
        arrays, n = gathered[level]
        shape = (owners * pair, 2, size, size)
        return call(
            f"narrow_{level}", narrow_body(n), {"gathered": arrays, "after": after},
            makes={"shared": VMEM(shape, BF16)},
            scratch={"near": VMEM(shape, F32), "sems": dma((owners * pair,))},
        )["shared"]

    sent = call(
        "send_level_0", send_body, {"residual": residual_in, "diag_inverse": diag_inverse},
        makes={"messages": messages},
        scratch={"near": VMEM(residual_in.shape, F32), "inverse": VMEM((size, size), BF16), "sems": dma((2,))},
    )["messages"]
    constants = call(
        "hold_blocks", hold_body, {"listed": column_lists.reshape(-1), **far_blocks},
        makes={
            "lists": SMEM((column_lists.size,), jnp.int32),
            "inverses": VMEM((levels, size, size), BF16),
            "lowers": VMEM((levels - 1, blocks, size, size), BF16),
        },
        scratch={"sems": dma((2,))},
        cost=pl.CostEstimate(flops=0, bytes_accessed=16 * 2**20, transcendentals=0),
    )
    received = to_all(sent)
    state = call(
        "forward_1", receive_body, {**constants, "received": received},
        makes={"source": own_rows, "finished": all_rows, "solved": rows},
    )
    source, finished, solved = state["source"], state["finished"], state["solved"]

    shared = {}
    level = 2
    accumulated = answers = products_sent = None
    while level < levels:
        arrived = exchange(solved)
        reads = {**constants, "source": source, **arrived}
        everywhere = level in shared_forward
        if everywhere:
            shared[level] = shared_of(level, solved)
            reads |= {"shared": shared[level], "received": received}
        last = level + everywhere == levels - 1

        def body(r, level=level, everywhere=everywhere, last=last):
            take_finished(r, level - 1)
            if everywhere:
                all_forward(r, level)
            answer = own_forward(r, level + everywhere)
            if last:
                r.accumulated[...] = jnp.zeros_like(r.accumulated)
                r.answers[...] = jnp.zeros_like(r.answers)
                own_products(r, levels - 1, own_backward(r, levels - 1))
            else:
                r.solved[...] = answer

        makes = {"accumulated": all_rows, "answers": own_rows, "sent": products} if last else {"solved": rows}
        state = call(f"forward_{level}", body, reads, {"finished": finished}, makes)
        finished, solved = state["finished"], state.get("solved")
        level += 1 + everywhere
    accumulated, answers, products_sent = state["accumulated"], state["answers"], state["sent"]

    level = levels - 2
    while level > 0:
        arrived = exchange(products_sent)
        reads = {**constants, "finished": finished, **arrived}
        everywhere = level in shared_levels
        if everywhere:
            if level not in shared:
                shared[level] = shared_of(level, products_sent)
            reads["shared"] = shared[level]
        last = level - everywhere == 1

        def body(r, level=level, everywhere=everywhere, last=last):
            take_products(r, level + 1)
            if everywhere:
                all_backward(r, level)
            if last:
                last_send(r)
            else:
                own = level - everywhere
                own_products(r, own, own_backward(r, own))

        state = call(
            f"backward_{level}", body, reads, {"accumulated": accumulated, "answers": answers},
            {"messages": messages} if last else {"sent": products},
            {"pieces": VMEM((owners, each, size), F32)} if last else {},
        )
        accumulated, answers, products_sent = state["accumulated"], state["answers"], state.get("sent")
        level -= 1 + everywhere
    return call(
        "backward_0", last_body,
        {"inverses": constants["inverses"], "received": to_all(state["messages"])},
        makes={"out": jax.ShapeDtypeStruct(residual_in.shape, F32)},
    )["out"]


def solution(mesh):
    placed = (
        P(None, "row", None, "col"),
        P(None, "row", None, None),
        P(None, "row", None, None, None),
        P(),
    )
    return jax.shard_map(
        shards, mesh=mesh, in_specs=placed, out_specs=P(None, "row", None, "col"), check_vma=False
    )
```

```python
import types

import jax
import jax.numpy as jnp
from jax import lax
from jax.experimental import pallas as pl
from jax.experimental.pallas import tpu as pltpu
from jax.sharding import PartitionSpec as P

VMEM = pltpu.VMEM
SMEM = pltpu.SMEM
F32 = jnp.float32
BF16 = jnp.bfloat16
CORES = 2
FAR = ("residual", "diag_inverse", "lower_blocks")


def two_parts(rows):
    high = rows.astype(BF16).astype(F32)
    return jnp.concatenate([high, rows - high], axis=0).astype(BF16)


def times(rows, block, transposed):
    contract = 1 if transposed else 0
    product = lax.dot_general(
        two_parts(rows), block, (((1,), (contract,)), ((), ())), preferred_element_type=F32
    )
    count = rows.shape[0]
    return product[:count] + product[count:]


def lane_group(shape, width):
    return lax.broadcasted_iota(jnp.int32, shape, 1) // width


def regroup(pieces, width):
    rows, size = pieces[0].shape
    groups = size // width
    stacked = jnp.concatenate(pieces, axis=0)
    rolled = [stacked if d == 0 else pltpu.roll(stacked, d * width, 1) for d in range(groups)]
    group = lane_group((rows, size), width)

    def result(b):
        total = jnp.zeros((rows, size), F32)
        for a in range(len(pieces)):
            moved = rolled[(a - b) % groups][a * rows : (a + 1) * rows]
            total = jnp.where(group == a, moved, total)
        return total

    return result


def regroup_one(pieces, width, b):
    rows, size = pieces[0].shape
    groups = size // width
    group = lane_group((rows, size), width)
    total = jnp.zeros((rows, size), F32)
    for a, piece in enumerate(pieces):
        shift = (a - b) % groups
        total = jnp.where(group == a, pltpu.roll(piece, shift * width, 1) if shift else piece, total)
    return total


def routes(count):
    order = [mask for mask in (1, 3, 2) if mask < count] + list(range(4, count))
    return [tuple(order[i : i + 2]) for i in range(0, len(order) - 1, 2)], order[-1]


def placed_in(key, array):
    if key == "listed":
        return array
    space = SMEM if key == "lists" else pltpu.HBM if key in FAR else VMEM
    return pltpu.with_memory_space_constraint(array, space)


def call(name, body, reads, updates=None, makes=None, scratch=None, cost=None):
    updates, makes, scratch = updates or {}, makes or {}, scratch or {}
    ins = {**reads, **updates}
    outs = {key: VMEM(value.shape, value.dtype) for key, value in updates.items()} | makes
    in_names, out_names, scratch_names = list(ins), list(outs), list(scratch)

    def kernel(*refs):
        space = types.SimpleNamespace()
        for key, ref in zip(in_names + out_names + scratch_names, refs, strict=True):
            setattr(space, key, ref)
        column = lax.axis_index("col")
        space.row, space.z, space.core = lax.axis_index("row"), lax.div(column, CORES), lax.rem(column, CORES)
        body(space)

    def spec(key):
        if key in ("lists", "listed"):
            return pl.BlockSpec(memory_space=SMEM)
        return pl.BlockSpec(memory_space=pltpu.HBM if key in FAR else VMEM)

    results = pl.pallas_call(
        kernel,
        in_specs=[spec(key) for key in in_names],
        out_specs=[spec(key) for key in out_names],
        out_shape=[outs[key] for key in out_names],
        input_output_aliases={in_names.index(key): out_names.index(key) for key in updates},
        scratch_shapes=list(scratch.values()),
        compiler_params=pltpu.CompilerParams(vmem_limit_bytes=24 * 2**20),
        cost_estimate=cost,
        name=name,
    )(*[placed_in(key, value) for key, value in ins.items()])
    return dict(zip(out_names, results, strict=True))


def shards(residual_in, diag_inverse, lower_blocks, column_lists):
    levels, _, probes, width = residual_in.shape
    size = diag_inverse.shape[-1]
    owners, columns = lax.axis_size("row"), lax.axis_size("col")
    layers = columns // CORES
    each = probes // layers
    blocks = column_lists.shape[2]
    rows = VMEM((each, size), F32)
    own_rows = VMEM((levels, each, size), F32)
    all_rows = VMEM((levels * owners, each, size), F32)
    packed_rows = VMEM((columns, each, size), F32)
    row_routes, layer_routes = routes(owners), routes(layers)
    dma = pltpu.SemaphoreType.DMA

    def swap(array):
        return lax.ppermute(array, "col", [(c, c ^ 1) for c in range(columns)])

    def exchange(axis, paired, single):
        pairs, last = row_routes if axis == "row" else layer_routes

        def send(array, masks):
            steps = []
            for row in range(owners):
                for column in range(columns):
                    mask = masks[column % CORES]
                    to = (row ^ mask, column) if axis == "row" else (row, column ^ (CORES * mask))
                    steps.append((row * columns + column, to[0] * columns + to[1]))
            return lax.ppermute(array, ("row", "col"), steps)

        got = {}
        for i, masks in enumerate(pairs):
            got[f"direct_{i}"] = send(paired[i], masks)
        got["single"] = send(single, (last, last))
        for i in range(len(pairs)):
            got[f"passed_{i}"] = swap(got[f"direct_{i}"])
        return got

    def partners(r, axis):
        pairs, last = row_routes if axis == "row" else layer_routes
        here = r.row if axis == "row" else r.z
        found = []
        for i, (one, other) in enumerate(pairs):
            found.append((f"direct_{i}", here ^ jnp.where(r.core == 0, one, other)))
            found.append((f"passed_{i}", here ^ jnp.where(r.core == 0, other, one)))
        return found + [("single", here ^ last)]

    def outgoing(r, axis):
        return [(f"to_{name}", to) for name, to in partners(r, axis) if not name.startswith("passed")]

    def exchanged(axis, state):
        pairs, _ = row_routes if axis == "row" else layer_routes
        return exchange(axis, [state[f"to_direct_{i}"] for i in range(len(pairs))], state["to_single"])

    def messages(axis, paired, single):
        pairs, _ = row_routes if axis == "row" else layer_routes
        return {f"to_direct_{i}": VMEM(paired, F32) for i in range(len(pairs))} | {"to_single": VMEM(single, F32)}

    def column_of(r, level, k):
        return r.lists[((level - 1) * owners + r.row) * blocks + k]

    def chip_rows(z):
        return pl.ds(pl.multiple_of(z * each, each), each)

    def pack_body(r):
        copy = pltpu.make_async_copy(r.residual, r.near, r.sems.at[0])
        copy.start()
        copy.wait()
        total = jnp.zeros((probes, size), F32)
        for level in range(levels):
            wide = jnp.concatenate([r.near[level, 0], jnp.zeros((probes, size - width), F32)], axis=1)
            total = total + (pltpu.roll(wide, level * width, 1) if level else wide)
        r.packed[...] = total

    def spread_body(r):
        for name, z in outgoing(r, "layer"):
            message = getattr(r, name)
            message[r.core] = r.packed[chip_rows(z)]
            message[1 - r.core] = r.other[chip_rows(z)]

    def hold_body(r):
        first = pltpu.make_async_copy(r.diag_inverse.at[:, 0], r.inverses, r.sems.at[0])
        second = pltpu.make_async_copy(r.lower_blocks.at[:, 0], r.lowers, r.sems.at[1])
        first.start()
        second.start()
        for i in range(r.lists.shape[0]):
            r.lists[i] = r.listed[i]
        first.wait()
        second.wait()

    def begin_body(r):
        r.pieces[CORES * r.z + r.core] = r.packed[chip_rows(r.z)]
        r.pieces[CORES * r.z + 1 - r.core] = r.other[chip_rows(r.z)]
        for name, z in partners(r, "layer"):
            for core in range(CORES):
                r.pieces[CORES * z + core] = getattr(r, name)[core]
        answer = times(regroup_one([r.pieces[c] for c in range(columns)], width, 0), r.inverses[0], True)
        r.finished[r.row] = answer
        r.solved[...] = answer

    def source_body(r):
        moved = regroup([r.pieces[c] for c in range(columns)], width)
        for level in range(1, levels):
            r.source[level] = moved(level)

    def forward_body(level):
        def body(r):
            for name, owner in partners(r, "row"):
                r.finished[(level - 1) * owners + owner] = getattr(r, name)[...]
            total = r.source[level]
            for k in range(blocks):
                total = total - times(r.finished[column_of(r, level, k)], r.lowers[level - 1, k], True)
            answer = times(total, r.inverses[level], True)
            r.finished[level * owners + r.row] = answer
            if level < levels - 1:
                r.solved[...] = answer
            else:
                r.accumulated[...] = jnp.zeros_like(r.accumulated)
                r.answers[...] = jnp.zeros_like(r.answers)
                backward(r, level, answer)

        return body

    def backward(r, level, source):
        answer = times(source, r.inverses[level], False)
        r.answers[level] = answer
        for k in range(blocks):
            r.accumulated[column_of(r, level, k)] += times(answer, r.lowers[level - 1, k], False)
        for name, owner in outgoing(r, "row"):
            getattr(r, name)[...] = r.accumulated[(level - 1) * owners + owner]

    def source_of(r, level):
        row = level * owners + r.row
        total = r.finished[row] - r.accumulated[row]
        for name, _ in partners(r, "row"):
            total = total - getattr(r, name)[...]
        return total

    def last_body(r):
        r.answers[0] = times(source_of(r, 0), r.inverses[0], False)
        moved = regroup([r.answers[level] for level in range(levels)], width)
        for column in range(columns):
            r.pieces[column] = moved(column)
        for name, z in outgoing(r, "layer"):
            if name == "to_single":
                r.to_single[...] = r.pieces[CORES * z + r.core]
            else:
                for core in range(CORES):
                    getattr(r, name)[core] = r.pieces[CORES * z + core]
        r.kept[...] = r.pieces[CORES * r.z + r.core]

    def out_body(r):
        r.whole[chip_rows(r.z)] = r.kept[...]
        for name, z in partners(r, "layer"):
            message = getattr(r, name)
            r.whole[chip_rows(z)] = message[...] if name == "single" else message[r.core]
        whole = r.whole[...]
        for level in range(levels):
            moved = pltpu.roll(whole, size - level * width, 1) if level else whole
            r.out[level, 0] = moved[:, :width]

    packed = call(
        "pack", pack_body, {"residual": residual_in}, makes={"packed": VMEM((probes, size), F32)},
        scratch={"near": VMEM(residual_in.shape, F32), "sems": dma((1,))},
    )["packed"]
    other = swap(packed)
    held = call(
        "hold_blocks", hold_body,
        {"listed": column_lists.reshape(-1), "diag_inverse": diag_inverse, "lower_blocks": lower_blocks},
        makes={
            "lists": SMEM((column_lists.size,), jnp.int32),
            "inverses": VMEM((levels, size, size), BF16),
            "lowers": VMEM((levels - 1, blocks, size, size), BF16),
        },
        scratch={"sems": dma((2,))},
        cost=pl.CostEstimate(flops=0, bytes_accessed=16 * 2**20, transcendentals=0),
    )
    both = (CORES, each, size)
    spread = call("spread", spread_body, {"packed": packed, "other": other}, makes=messages("layer", both, both))
    begun = call(
        "forward_0", begin_body,
        {"packed": packed, "other": other, "inverses": held["inverses"], **exchanged("layer", spread)},
        makes={"pieces": packed_rows, "finished": all_rows, "solved": rows},
    )
    source = call("source", source_body, {"pieces": begun["pieces"]}, makes={"source": own_rows})["source"]
    finished, solved = begun["finished"], begun["solved"]
    to_owners = messages("row", (each, size), (each, size))
    for level in range(1, levels):
        last = level == levels - 1
        state = call(
            f"forward_{level}", forward_body(level),
            {**held, "source": source, **exchange("row", [solved] * len(row_routes[0]), solved)},
            {"finished": finished},
            {"accumulated": all_rows, "answers": own_rows, **to_owners} if last else {"solved": rows},
        )
        finished, solved = state["finished"], state.get("solved")
    for level in reversed(range(1, levels - 1)):
        state = call(
            f"backward_{level}", lambda r, level=level: backward(r, level, source_of(r, level)),
            {**held, "finished": finished, **exchanged("row", state)},
            {"accumulated": state["accumulated"], "answers": state["answers"]}, to_owners,
        )
    ended = call(
        "backward_0", last_body,
        {
            "inverses": held["inverses"], "finished": finished, "accumulated": state["accumulated"],
            **exchanged("row", state),
        },
        {"answers": state["answers"]},
        {"kept": rows, **messages("layer", both, (each, size))},
        {"pieces": packed_rows},
    )
    return call(
        "out", out_body, {"kept": ended["kept"], **exchanged("layer", ended)},
        makes={"out": jax.ShapeDtypeStruct(residual_in.shape, F32)},
        scratch={"whole": VMEM((probes, size), F32)},
    )["out"]


def solution(mesh):
    placed = (
        P(None, "row", None, "col"),
        P(None, "row", None, None),
        P(None, "row", None, None, None),
        P(),
    )
    return jax.shard_map(
        shards, mesh=mesh, in_specs=placed, out_specs=P(None, "row", None, "col"), check_vma=False
    )
```

```python
import types

import jax
import jax.numpy as jnp
from jax import lax
from jax.experimental import pallas as pl
from jax.experimental.pallas import tpu as pltpu
from jax.sharding import PartitionSpec as P

VMEM = pltpu.VMEM
SMEM = pltpu.SMEM
F32 = jnp.float32
BF16 = jnp.bfloat16
CORES = 2
FAR = ("residual", "diag_inverse", "lower_blocks", "listed")


def two_parts(rows):
    high = rows.astype(BF16).astype(F32)
    return jnp.concatenate([high, rows - high], axis=0).astype(BF16)


def times(rows, block, transposed):
    contract = 1 if transposed else 0
    product = lax.dot_general(
        two_parts(rows), block, (((1,), (contract,)), ((), ())), preferred_element_type=F32
    )
    count = rows.shape[0]
    return product[:count] + product[count:]


def lane_group(shape, width):
    return lax.broadcasted_iota(jnp.int32, shape, 1) // width


def regroup(pieces, width):
    rows, size = pieces[0].shape
    groups = size // width
    stacked = jnp.concatenate(pieces, axis=0)
    rolled = [stacked if d == 0 else pltpu.roll(stacked, d * width, 1) for d in range(groups)]
    group = lane_group((rows, size), width)

    def result(b):
        total = jnp.zeros((rows, size), F32)
        for a in range(len(pieces)):
            moved = rolled[(a - b) % groups][a * rows : (a + 1) * rows]
            total = jnp.where(group == a, moved, total)
        return total

    return result


def regroup_one(pieces, width, b):
    rows, size = pieces[0].shape
    groups = size // width
    group = lane_group((rows, size), width)
    total = jnp.zeros((rows, size), F32)
    for a, piece in enumerate(pieces):
        shift = (a - b) % groups
        total = jnp.where(group == a, pltpu.roll(piece, shift * width, 1) if shift else piece, total)
    return total


def routes(count):
    order = [mask for mask in (1, 3, 2) if mask < count] + list(range(4, count))
    return [tuple(order[i : i + 2]) for i in range(0, len(order) - 1, 2)], order[-1]


def placed_in(key, array):
    space = SMEM if key == "lists" else pltpu.HBM if key in FAR else VMEM
    return pltpu.with_memory_space_constraint(array, space)


def call(name, body, reads, updates=None, makes=None, scratch=None, cost=None):
    updates, makes, scratch = updates or {}, makes or {}, scratch or {}
    ins = {**reads, **updates}
    outs = {key: VMEM(value.shape, value.dtype) for key, value in updates.items()} | makes
    in_names, out_names, scratch_names = list(ins), list(outs), list(scratch)

    def kernel(*refs):
        space = types.SimpleNamespace()
        for key, ref in zip(in_names + out_names + scratch_names, refs, strict=True):
            setattr(space, key, ref)
        column = lax.axis_index("col")
        space.row, space.z, space.core = lax.axis_index("row"), lax.div(column, CORES), lax.rem(column, CORES)
        body(space)

    def spec(key):
        if key in ("lists", "listed"):
            return pl.BlockSpec(memory_space=SMEM)
        return pl.BlockSpec(memory_space=pltpu.HBM if key in FAR else VMEM)

    results = pl.pallas_call(
        kernel,
        in_specs=[spec(key) for key in in_names],
        out_specs=[spec(key) for key in out_names],
        out_shape=[outs[key] for key in out_names],
        input_output_aliases={in_names.index(key): out_names.index(key) for key in updates},
        scratch_shapes=list(scratch.values()),
        compiler_params=pltpu.CompilerParams(vmem_limit_bytes=24 * 2**20),
        cost_estimate=cost,
        name=name,
    )(*[placed_in(key, value) for key, value in ins.items()])
    return dict(zip(out_names, results, strict=True))


def shards(residual_in, diag_inverse, lower_blocks, column_lists):
    levels, _, probes, width = residual_in.shape
    size = diag_inverse.shape[-1]
    owners, columns = lax.axis_size("row"), lax.axis_size("col")
    layers = columns // CORES
    each = probes // layers
    blocks = column_lists.shape[2]
    rows = VMEM((each, size), F32)
    own_rows = VMEM((levels, each, size), F32)
    all_rows = VMEM((levels * owners, each, size), F32)
    packed_rows = VMEM((columns, each, size), F32)
    row_routes, layer_routes = routes(owners), routes(layers)
    dma = pltpu.SemaphoreType.DMA

    def swap(array):
        return lax.ppermute(array, "col", [(c, c ^ 1) for c in range(columns)])

    def exchange(axis, paired, single):
        pairs, last = row_routes if axis == "row" else layer_routes

        def send(array, masks):
            steps = []
            for row in range(owners):
                for column in range(columns):
                    mask = masks[column % CORES]
                    to = (row ^ mask, column) if axis == "row" else (row, column ^ (CORES * mask))
                    steps.append((row * columns + column, to[0] * columns + to[1]))
            return lax.ppermute(array, ("row", "col"), steps)

        got = {}
        for i, masks in enumerate(pairs):
            got[f"direct_{i}"] = send(paired[i], masks)
        got["single"] = send(single, (last, last))
        for i in range(len(pairs)):
            got[f"passed_{i}"] = swap(got[f"direct_{i}"])
        return got

    def partners(r, axis):
        pairs, last = row_routes if axis == "row" else layer_routes
        here = r.row if axis == "row" else r.z
        found = []
        for i, (one, other) in enumerate(pairs):
            found.append((f"direct_{i}", here ^ jnp.where(r.core == 0, one, other)))
            found.append((f"passed_{i}", here ^ jnp.where(r.core == 0, other, one)))
        return found + [("single", here ^ last)]

    def outgoing(r, axis):
        return [(f"to_{name}", to) for name, to in partners(r, axis) if not name.startswith("passed")]

    def exchanged(axis, state):
        pairs, _ = row_routes if axis == "row" else layer_routes
        return exchange(axis, [state[f"to_direct_{i}"] for i in range(len(pairs))], state["to_single"])

    def messages(axis, paired, single):
        pairs, _ = row_routes if axis == "row" else layer_routes
        return {f"to_direct_{i}": VMEM(paired, F32) for i in range(len(pairs))} | {"to_single": VMEM(single, F32)}

    def column_of(r, level, k):
        return r.lists[((level - 1) * owners + r.row) * blocks + k]

    def chip_rows(z):
        return pl.ds(pl.multiple_of(z * each, each), each)

    def packed(residual):
        total = jnp.zeros((probes, size), F32)
        for level in range(levels):
            wide = jnp.concatenate([residual[level, 0], jnp.zeros((probes, size - width), F32)], axis=1)
            total = total + (pltpu.roll(wide, level * width, 1) if level else wide)
        return total

    def pack_body(r):
        copy = pltpu.make_async_copy(r.residual, r.near, r.sems.at[0])
        block = pltpu.make_async_copy(r.diag_inverse.at[0, 0], r.inverse_0, r.sems.at[1])
        copy.start()
        block.start()
        copy.wait()
        r.packed[...] = packed(r.near)
        block.wait()

    def spread_body(r):
        r.other[...] = packed(r.passed)
        for name, z in outgoing(r, "layer"):
            message = getattr(r, name)
            message[r.core] = r.packed[chip_rows(z)]
            message[1 - r.core] = r.other[chip_rows(z)]

    def lists_body(r):
        for level in range(levels - 1):
            for owner in range(owners):
                for k in range(blocks):
                    r.lists[(level * owners + owner) * blocks + k] = r.listed[k, owner, level]

    def hold_body(r):
        first = pltpu.make_async_copy(r.diag_inverse.at[:, 0], r.inverses, r.sems.at[0])
        second = pltpu.make_async_copy(r.lower_blocks.at[:1, 0], r.lowers_1, r.sems.at[1])
        first.start()
        second.start()
        first.wait()
        second.wait()

    def hold_part_body(part):
        def body(r):
            source = r.lower_blocks.at[part[0] - 1 : part[-1], 0]
            copy = pltpu.make_async_copy(source, getattr(r, f"lowers_{part[0]}"), r.sems.at[0])
            copy.start()
            copy.wait()

        return body

    parts = [range(1, 2), range(2, levels // 2 + 1), range(levels // 2 + 1, levels)]

    def lower(r, level, k):
        part = next(part for part in parts if level in part)
        return getattr(r, f"lowers_{part[0]}")[level - part[0], k]

    def begin_body(r):
        r.pieces[CORES * r.z + r.core] = r.packed[chip_rows(r.z)]
        r.pieces[CORES * r.z + 1 - r.core] = r.other[chip_rows(r.z)]
        for name, z in partners(r, "layer"):
            for core in range(CORES):
                r.pieces[CORES * z + core] = getattr(r, name)[core]
        answer = times(regroup_one([r.pieces[c] for c in range(columns)], width, 0), r.inverse_0[...], True)
        r.finished[r.row] = answer
        r.solved[...] = answer

    def source_body(r):
        moved = regroup([r.pieces[c] for c in range(columns)], width)
        for level in range(1, levels):
            r.source[level] = moved(level)

    def forward_body(level):
        def body(r):
            for name, owner in partners(r, "row"):
                r.finished[(level - 1) * owners + owner] = getattr(r, name)[...]
            total = r.source[level]
            for k in range(blocks):
                total = total - times(r.finished[column_of(r, level, k)], lower(r, level, k), True)
            answer = times(total, r.inverses[level], True)
            r.finished[level * owners + r.row] = answer
            if level < levels - 1:
                r.solved[...] = answer
            else:
                r.accumulated[...] = jnp.zeros_like(r.accumulated)
                r.answers[...] = jnp.zeros_like(r.answers)
                backward(r, level, answer)

        return body

    def backward(r, level, source):
        answer = times(source, r.inverses[level], False)
        r.answers[level] = answer
        for k in range(blocks):
            r.accumulated[column_of(r, level, k)] += times(answer, lower(r, level, k), False)
        for name, owner in outgoing(r, "row"):
            getattr(r, name)[...] = r.accumulated[(level - 1) * owners + owner]

    def source_of(r, level):
        row = level * owners + r.row
        total = r.finished[row] - r.accumulated[row]
        for name, _ in partners(r, "row"):
            total = total - getattr(r, name)[...]
        return total

    def last_body(r):
        r.answers[0] = times(source_of(r, 0), r.inverses[0], False)
        moved = regroup([r.answers[level] for level in range(levels)], width)
        for column in range(columns):
            r.pieces[column] = moved(column)
        for name, z in outgoing(r, "layer"):
            for core in range(CORES):
                getattr(r, name)[core] = r.pieces[CORES * z + core]
        r.kept[...] = r.pieces[CORES * r.z + r.core]

    def out_body(r):
        r.whole[chip_rows(r.z)] = r.kept[...]
        for name, z in partners(r, "layer"):
            r.whole[chip_rows(z)] = getattr(r, name)[r.core]
        whole = r.whole[...]
        for level in range(levels):
            moved = pltpu.roll(whole, size - level * width, 1) if level else whole
            r.out[level, 0] = moved[:, :width]

    blocks_in = {"diag_inverse": diag_inverse, "lower_blocks": lower_blocks}
    begun = call(
        "pack", pack_body, {"residual": residual_in, "diag_inverse": diag_inverse},
        makes={"packed": VMEM((probes, size), F32), "inverse_0": VMEM((size, size), BF16)},
        scratch={"near": VMEM(residual_in.shape, F32), "sems": dma((2,))},
    )
    both = (CORES, each, size)
    spread = call(
        "spread", spread_body, {"packed": begun["packed"], "passed": swap(residual_in)},
        makes={"other": VMEM((probes, size), F32), **messages("layer", both, both)},
    )
    arrived = exchanged("layer", spread)
    lists = call(
        "lists", lists_body, {"listed": column_lists.transpose(2, 1, 0), "after": arrived["direct_0"]},
        makes={"lists": SMEM((column_lists.size,), jnp.int32)},
    )["lists"]
    begun = call(
        "forward_0", begin_body,
        {
            "packed": begun["packed"], "other": spread["other"], "inverse_0": begun["inverse_0"], "lists": lists,
            **arrived,
        },
        makes={"pieces": packed_rows, "finished": all_rows, "solved": rows},
    )
    held = {"lists": lists} | call(
        "hold", hold_body, {**blocks_in, "after": begun["solved"]},
        makes={"inverses": VMEM((levels, size, size), BF16), "lowers_1": VMEM((1, blocks, size, size), BF16)},
        scratch={"sems": dma((2,))},
    )
    source = call("source", source_body, {"pieces": begun["pieces"]}, makes={"source": own_rows})["source"]
    finished, solved = begun["finished"], begun["solved"]
    to_owners = messages("row", (each, size), (each, size))
    for level in range(1, levels):
        last = level == levels - 1
        if level in (2, 3):
            part = parts[level - 1]
            held |= call(
                f"hold_{level}", hold_part_body(part), {"lower_blocks": lower_blocks, "after": solved},
                makes={f"lowers_{part[0]}": VMEM((len(part), blocks, size, size), BF16)},
                scratch={"sems": dma((1,))},
            )
        state = call(
            f"forward_{level}", forward_body(level),
            {**held, "source": source, **exchange("row", [solved] * len(row_routes[0]), solved)},
            {"finished": finished},
            {"accumulated": all_rows, "answers": own_rows, **to_owners} if last else {"solved": rows},
        )
        finished, solved = state["finished"], state.get("solved")
    for level in reversed(range(1, levels - 1)):
        state = call(
            f"backward_{level}", lambda r, level=level: backward(r, level, source_of(r, level)),
            {**held, "finished": finished, **exchanged("row", state)},
            {"accumulated": state["accumulated"], "answers": state["answers"]}, to_owners,
        )
    ended = call(
        "backward_0", last_body,
        {
            "inverses": held["inverses"], "finished": finished, "accumulated": state["accumulated"],
            **exchanged("row", state),
        },
        {"answers": state["answers"]},
        {"kept": rows, **messages("layer", both, both)},
        {"pieces": packed_rows},
    )
    return call(
        "out", out_body, {"kept": ended["kept"], **exchanged("layer", ended)},
        makes={"out": jax.ShapeDtypeStruct(residual_in.shape, F32)},
        scratch={"whole": VMEM((probes, size), F32)},
    )["out"]


def solution(mesh):
    placed = (
        P(None, "row", None, "col"),
        P(None, "row", None, None),
        P(None, "row", None, None, None),
        P(),
    )
    return jax.shard_map(
        shards, mesh=mesh, in_specs=placed, out_specs=P(None, "row", None, "col"), check_vma=False
    )
```

```python
import types

import jax
import jax.numpy as jnp
from jax import lax
from jax.experimental import pallas as pl
from jax.experimental.pallas import tpu as pltpu
from jax.sharding import PartitionSpec as P

VMEM = pltpu.VMEM
SMEM = pltpu.SMEM
F32 = jnp.float32
BF16 = jnp.bfloat16
CORES = 2
FAR = ("residual", "diag_inverse", "lower_blocks", "listed")


def two_parts(rows):
    high = rows.astype(BF16).astype(F32)
    return jnp.concatenate([high, rows - high], axis=0).astype(BF16)


def times(rows, block, transposed):
    contract = 1 if transposed else 0
    product = lax.dot_general(
        two_parts(rows), block, (((1,), (contract,)), ((), ())), preferred_element_type=F32
    )
    count = rows.shape[0]
    return product[:count] + product[count:]


def lane_group(shape, width):
    return lax.broadcasted_iota(jnp.int32, shape, 1) // width


def regroup(pieces, width):
    rows, size = pieces[0].shape
    groups = size // width
    stacked = jnp.concatenate(pieces, axis=0)
    rolled = [stacked if d == 0 else pltpu.roll(stacked, d * width, 1) for d in range(groups)]
    group = lane_group((rows, size), width)

    def result(b):
        total = jnp.zeros((rows, size), F32)
        for a in range(len(pieces)):
            moved = rolled[(a - b) % groups][a * rows : (a + 1) * rows]
            total = jnp.where(group == a, moved, total)
        return total

    return result


def regroup_one(pieces, width, b):
    rows, size = pieces[0].shape
    groups = size // width
    group = lane_group((rows, size), width)
    total = jnp.zeros((rows, size), F32)
    for a, piece in enumerate(pieces):
        shift = (a - b) % groups
        total = jnp.where(group == a, pltpu.roll(piece, shift * width, 1) if shift else piece, total)
    return total


def routes(count):
    order = [mask for mask in (1, 3, 2) if mask < count] + list(range(4, count))
    return [tuple(order[i : i + 2]) for i in range(0, len(order) - 1, 2)], order[-1]


def placed_in(key, array):
    space = SMEM if key == "lists" else pltpu.HBM if key in FAR else VMEM
    return pltpu.with_memory_space_constraint(array, space)


def call(name, body, reads, updates=None, makes=None, scratch=None, cost=None):
    updates, makes, scratch = updates or {}, makes or {}, scratch or {}
    ins = {**reads, **updates}
    outs = {key: VMEM(value.shape, value.dtype) for key, value in updates.items()} | makes
    in_names, out_names, scratch_names = list(ins), list(outs), list(scratch)

    def kernel(*refs):
        space = types.SimpleNamespace()
        for key, ref in zip(in_names + out_names + scratch_names, refs, strict=True):
            setattr(space, key, ref)
        column = lax.axis_index("col")
        space.row, space.z, space.core = lax.axis_index("row"), lax.div(column, CORES), lax.rem(column, CORES)
        body(space)

    def spec(key):
        if key in ("lists", "listed"):
            return pl.BlockSpec(memory_space=SMEM)
        return pl.BlockSpec(memory_space=pltpu.HBM if key in FAR else VMEM)

    results = pl.pallas_call(
        kernel,
        in_specs=[spec(key) for key in in_names],
        out_specs=[spec(key) for key in out_names],
        out_shape=[outs[key] for key in out_names],
        input_output_aliases={in_names.index(key): out_names.index(key) for key in updates},
        scratch_shapes=list(scratch.values()),
        compiler_params=pltpu.CompilerParams(vmem_limit_bytes=24 * 2**20),
        cost_estimate=cost,
        name=name,
    )(*[placed_in(key, value) for key, value in ins.items()])
    return dict(zip(out_names, results, strict=True))


def shards(residual_in, diag_inverse, lower_blocks, column_lists):
    levels, _, probes, width = residual_in.shape
    size = diag_inverse.shape[-1]
    owners, columns = lax.axis_size("row"), lax.axis_size("col")
    layers = columns // CORES
    each = probes // layers
    blocks = column_lists.shape[2]
    rows = VMEM((each, size), F32)
    own_rows = VMEM((levels, each, size), F32)
    all_rows = VMEM((levels * owners, each, size), F32)
    packed_rows = VMEM((columns, each, size), F32)
    row_routes, layer_routes = routes(owners), routes(layers)
    dma = pltpu.SemaphoreType.DMA

    def swap(array):
        return lax.ppermute(array, "col", [(c, c ^ 1) for c in range(columns)])

    def exchange(axis, paired, single):
        pairs, last = row_routes if axis == "row" else layer_routes

        def send(array, masks):
            steps = []
            for row in range(owners):
                for column in range(columns):
                    mask = masks[column % CORES]
                    to = (row ^ mask, column) if axis == "row" else (row, column ^ (CORES * mask))
                    steps.append((row * columns + column, to[0] * columns + to[1]))
            return lax.ppermute(array, ("row", "col"), steps)

        got = {"single": send(single, (last, last))}
        for i, masks in enumerate(pairs):
            got[f"direct_{i}"] = send(paired[i], masks)
        for i in range(len(pairs)):
            got[f"passed_{i}"] = swap(got[f"direct_{i}"])
        return got

    def partners(r, axis):
        pairs, last = row_routes if axis == "row" else layer_routes
        here = r.row if axis == "row" else r.z
        found = []
        for i, (one, other) in enumerate(pairs):
            found.append((f"direct_{i}", here ^ jnp.where(r.core == 0, one, other)))
            found.append((f"passed_{i}", here ^ jnp.where(r.core == 0, other, one)))
        return found + [("single", here ^ last)]

    def outgoing(r, axis):
        return [(f"to_{name}", to) for name, to in partners(r, axis) if not name.startswith("passed")]

    def exchanged(axis, state):
        pairs, _ = row_routes if axis == "row" else layer_routes
        return exchange(axis, [state[f"to_direct_{i}"] for i in range(len(pairs))], state["to_single"])

    def messages(axis, paired, single):
        pairs, _ = row_routes if axis == "row" else layer_routes
        return {f"to_direct_{i}": VMEM(paired, F32) for i in range(len(pairs))} | {"to_single": VMEM(single, F32)}

    def column_of(r, level, k):
        return r.lists[((level - 1) * owners + r.row) * blocks + k]

    def chip_rows(z):
        return pl.ds(pl.multiple_of(z * each, each), each)

    def packed(residual):
        total = jnp.zeros((probes, size), F32)
        for level in range(levels):
            wide = jnp.concatenate([residual[level, 0], jnp.zeros((probes, size - width), F32)], axis=1)
            total = total + (pltpu.roll(wide, level * width, 1) if level else wide)
        return total

    def pack_body(r):
        copy = pltpu.make_async_copy(r.residual, r.near, r.sems.at[0])
        copy.start()
        block = pltpu.make_async_copy(r.diag_inverse.at[0, 0], r.inverse_0, r.sems.at[1])
        block.start()
        others = [
            pltpu.make_async_copy(r.diag_inverse.at[1, 0], r.inverse_1, r.sems.at[2]),
            pltpu.make_async_copy(r.lower_blocks.at[0, 0], r.lower_1, r.sems.at[3]),
        ]
        for other in others:
            other.start()
        copy.wait()
        r.packed[...] = packed(r.near)
        block.wait()
        for other in others:
            other.wait()

    def spread_body(r):
        r.other[...] = packed(r.passed)
        for name, z in outgoing(r, "layer"):
            message = getattr(r, name)
            message[r.core] = r.packed[chip_rows(z)]
            message[1 - r.core] = r.other[chip_rows(z)]

    def lists_body(r):
        for level in range(levels - 1):
            for owner in range(owners):
                for k in range(blocks):
                    r.lists[(level * owners + owner) * blocks + k] = r.listed[k, owner, level]

    def inverse(r, level):
        return r.inverse_1[...] if level == 1 else r.inverses[level, 0]

    def lower(r, level, k):
        return r.lower_1[k] if level == 1 else r.lowers[level - 1, 0, k]

    def begin_body(r):
        r.pieces[CORES * r.z + r.core] = r.packed[chip_rows(r.z)]
        r.pieces[CORES * r.z + 1 - r.core] = r.other[chip_rows(r.z)]
        for name, z in partners(r, "layer"):
            for core in range(CORES):
                r.pieces[CORES * z + core] = getattr(r, name)[core]
        answer = times(regroup_one([r.pieces[c] for c in range(columns)], width, 0), r.inverse_0[...], True)
        r.finished[r.row] = answer
        r.solved[...] = answer

    def source_body(r):
        moved = regroup([r.pieces[c] for c in range(columns)], width)
        for level in range(1, levels):
            r.source[level] = moved(level)

    def forward_body(level):
        def body(r):
            for name, owner in partners(r, "row"):
                r.finished[(level - 1) * owners + owner] = getattr(r, name)[...]
            total = r.source[level]
            for k in range(blocks):
                total = total - times(r.finished[column_of(r, level, k)], lower(r, level, k), True)
            answer = times(total, inverse(r, level), True)
            r.finished[level * owners + r.row] = answer
            if level < levels - 1:
                r.solved[...] = answer
            else:
                r.accumulated[...] = jnp.zeros_like(r.accumulated)
                r.answers[...] = jnp.zeros_like(r.answers)
                backward(r, level, answer)

        return body

    def backward(r, level, source):
        answer = times(source, inverse(r, level), False)
        r.answers[level] = answer
        for k in range(blocks):
            r.accumulated[column_of(r, level, k)] += times(answer, lower(r, level, k), False)
        for name, owner in outgoing(r, "row"):
            getattr(r, name)[...] = r.accumulated[(level - 1) * owners + owner]

    def source_of(r, level):
        row = level * owners + r.row
        total = r.finished[row] - r.accumulated[row]
        for name, _ in partners(r, "row"):
            total = total - getattr(r, name)[...]
        return total

    def last_body(r):
        r.answers[0] = times(source_of(r, 0), r.inverse_0[...], False)
        moved = regroup([r.answers[level] for level in range(levels)], width)
        for column in range(columns):
            r.pieces[column] = moved(column)
        for name, z in outgoing(r, "layer"):
            for core in range(CORES):
                getattr(r, name)[core] = r.pieces[CORES * z + core]
        r.kept[...] = r.pieces[CORES * r.z + r.core]

    def out_body(r):
        r.whole[chip_rows(r.z)] = r.kept[...]
        for name, z in partners(r, "layer"):
            r.whole[chip_rows(z)] = getattr(r, name)[r.core]
        whole = r.whole[...]
        for level in range(levels):
            moved = pltpu.roll(whole, size - level * width, 1) if level else whole
            r.out[level, 0] = moved[:, :width]

    blocks_in = {"diag_inverse": diag_inverse, "lower_blocks": lower_blocks}
    first_blocks = {"inverse_1": VMEM((size, size), BF16), "lower_1": VMEM((blocks, size, size), BF16)}
    at_start = call(
        "pack", pack_body, {"residual": residual_in, **blocks_in},
        makes={"packed": VMEM((probes, size), F32), "inverse_0": VMEM((size, size), BF16), **first_blocks},
        scratch={"near": VMEM(residual_in.shape, F32), "sems": dma((4,))},
    )
    both = (CORES, each, size)
    spread = call(
        "spread", spread_body, {"packed": at_start["packed"], "passed": swap(residual_in)},
        makes={"other": VMEM((probes, size), F32), **messages("layer", both, both)},
    )
    arrived = exchanged("layer", spread)
    lists = call(
        "lists", lists_body, {"listed": column_lists.transpose(2, 1, 0), "after": arrived["direct_0"]},
        makes={"lists": SMEM((column_lists.size,), jnp.int32)},
    )["lists"]
    begun = call(
        "forward_0", begin_body,
        {
            "packed": at_start["packed"], "other": spread["other"], "inverse_0": at_start["inverse_0"], "lists": lists,
            **arrived,
        },
        makes={"pieces": packed_rows, "finished": all_rows, "solved": rows},
    )
    held = {1: {key: at_start[key] for key in first_blocks}}
    source = call("source", source_body, {"pieces": begun["pieces"]}, makes={"source": own_rows})["source"]
    finished, solved = begun["finished"], begun["solved"]
    to_owners = messages("row", (each, size), (each, size))
    for level in range(1, levels):
        last = level == levels - 1
        arrived = exchange("row", [solved] * len(row_routes[0]), solved)
        held.setdefault(level, {"inverses": diag_inverse, "lowers": lower_blocks})
        state = call(
            f"forward_{level}", forward_body(level),
            {"lists": lists, **held[level], "source": source, **arrived},
            {"finished": finished},
            {"accumulated": all_rows, "answers": own_rows, **to_owners} if last else {"solved": rows},
        )
        finished, solved = state["finished"], state.get("solved")
    for level in reversed(range(1, levels - 1)):
        state = call(
            f"backward_{level}", lambda r, level=level: backward(r, level, source_of(r, level)),
            {"lists": lists, **held[level], "finished": finished, **exchanged("row", state)},
            {"accumulated": state["accumulated"], "answers": state["answers"]}, to_owners,
        )
    ended = call(
        "backward_0", last_body,
        {
            "inverse_0": at_start["inverse_0"], "finished": finished, "accumulated": state["accumulated"],
            **exchanged("row", state),
        },
        {"answers": state["answers"]},
        {"kept": rows, **messages("layer", both, both)},
        {"pieces": packed_rows},
    )
    return call(
        "out", out_body, {"kept": ended["kept"], **exchanged("layer", ended)},
        makes={"out": jax.ShapeDtypeStruct(residual_in.shape, F32)},
        scratch={"whole": VMEM((probes, size), F32)},
    )["out"]


def solution(mesh):
    placed = (
        P(None, "row", None, "col"),
        P(None, "row", None, None),
        P(None, "row", None, None, None),
        P(),
    )
    return jax.shard_map(
        shards, mesh=mesh, in_specs=placed, out_specs=P(None, "row", None, "col"), check_vma=False
    )
```

```python
import types

import jax
import jax.numpy as jnp
from jax import lax
from jax.experimental import pallas as pl
from jax.experimental.pallas import tpu as pltpu
from jax.sharding import PartitionSpec as P

VMEM = pltpu.VMEM
SMEM = pltpu.SMEM
F32 = jnp.float32
BF16 = jnp.bfloat16
CORES = 2
FAR = ("residual", "diag_inverse", "lower_blocks", "listed")


def two_parts(rows):
    high = rows.astype(BF16).astype(F32)
    return jnp.concatenate([high, rows - high], axis=0).astype(BF16)


def times(rows, block, transposed):
    contract = 1 if transposed else 0
    product = lax.dot_general(
        two_parts(rows), block, (((1,), (contract,)), ((), ())), preferred_element_type=F32
    )
    count = rows.shape[0]
    return product[:count] + product[count:]


def lane_group(shape, width):
    return lax.broadcasted_iota(jnp.int32, shape, 1) // width


def regroup(pieces, width):
    rows, size = pieces[0].shape
    groups = size // width
    stacked = jnp.concatenate(pieces, axis=0)
    rolled = [stacked if d == 0 else pltpu.roll(stacked, d * width, 1) for d in range(groups)]
    group = lane_group((rows, size), width)

    def result(b):
        total = jnp.zeros((rows, size), F32)
        for a in range(len(pieces)):
            moved = rolled[(a - b) % groups][a * rows : (a + 1) * rows]
            total = jnp.where(group == a, moved, total)
        return total

    return result


def regroup_one(pieces, width, b):
    rows, size = pieces[0].shape
    groups = size // width
    group = lane_group((rows, size), width)
    total = jnp.zeros((rows, size), F32)
    for a, piece in enumerate(pieces):
        shift = (a - b) % groups
        total = jnp.where(group == a, pltpu.roll(piece, shift * width, 1) if shift else piece, total)
    return total


def routes(count):
    order = [mask for mask in (1, 3, 2) if mask < count] + list(range(4, count))
    return [tuple(order[i : i + 2]) for i in range(0, len(order) - 1, 2)], order[-1]


def placed_in(key, array):
    space = SMEM if key == "lists" else pltpu.HBM if key in FAR else VMEM
    return pltpu.with_memory_space_constraint(array, space)


def call(name, body, reads, updates=None, makes=None, scratch=None, cost=None):
    updates, makes, scratch = updates or {}, makes or {}, scratch or {}
    ins = {**reads, **updates}
    outs = {key: VMEM(value.shape, value.dtype) for key, value in updates.items()} | makes
    in_names, out_names, scratch_names = list(ins), list(outs), list(scratch)

    def kernel(*refs):
        space = types.SimpleNamespace()
        for key, ref in zip(in_names + out_names + scratch_names, refs, strict=True):
            setattr(space, key, ref)
        column = lax.axis_index("col")
        space.row, space.z, space.core = lax.axis_index("row"), lax.div(column, CORES), lax.rem(column, CORES)
        body(space)

    def spec(key):
        if key in ("lists", "listed"):
            return pl.BlockSpec(memory_space=SMEM)
        return pl.BlockSpec(memory_space=pltpu.HBM if key in FAR else VMEM)

    results = pl.pallas_call(
        kernel,
        in_specs=[spec(key) for key in in_names],
        out_specs=[spec(key) for key in out_names],
        out_shape=[outs[key] for key in out_names],
        input_output_aliases={in_names.index(key): out_names.index(key) for key in updates},
        scratch_shapes=list(scratch.values()),
        compiler_params=pltpu.CompilerParams(vmem_limit_bytes=24 * 2**20),
        cost_estimate=cost,
        name=name,
    )(*[placed_in(key, value) for key, value in ins.items()])
    return dict(zip(out_names, results, strict=True))


def shards(residual_in, diag_inverse, lower_blocks, column_lists):
    levels, _, probes, width = residual_in.shape
    size = diag_inverse.shape[-1]
    owners, columns = lax.axis_size("row"), lax.axis_size("col")
    layers = columns // CORES
    each = probes // layers
    blocks = column_lists.shape[2]
    rows = VMEM((each, size), F32)
    own_rows = VMEM((levels, each, size), F32)
    all_rows = VMEM((levels * owners, each, size), F32)
    packed_rows = VMEM((columns, each, size), F32)
    row_routes, layer_routes = routes(owners), routes(layers)
    dma = pltpu.SemaphoreType.DMA

    def swap(array):
        return lax.ppermute(array, "col", [(c, c ^ 1) for c in range(columns)])

    def exchange(axis, paired, single):
        pairs, last = row_routes if axis == "row" else layer_routes

        def send(array, masks):
            steps = []
            for row in range(owners):
                for column in range(columns):
                    mask = masks[column % CORES]
                    to = (row ^ mask, column) if axis == "row" else (row, column ^ (CORES * mask))
                    steps.append((row * columns + column, to[0] * columns + to[1]))
            return lax.ppermute(array, ("row", "col"), steps)

        got = {"single": send(single, (last, last))}
        for i, masks in enumerate(pairs):
            got[f"direct_{i}"] = send(paired[i], masks)
        for i in range(len(pairs)):
            got[f"passed_{i}"] = swap(got[f"direct_{i}"])
        return got

    def partners(r, axis):
        pairs, last = row_routes if axis == "row" else layer_routes
        here = r.row if axis == "row" else r.z
        found = []
        for i, (one, other) in enumerate(pairs):
            found.append((f"direct_{i}", here ^ jnp.where(r.core == 0, one, other)))
            found.append((f"passed_{i}", here ^ jnp.where(r.core == 0, other, one)))
        return found + [("single", here ^ last)]

    def outgoing(r, axis):
        return [(f"to_{name}", to) for name, to in partners(r, axis) if not name.startswith("passed")]

    def exchanged(axis, state):
        pairs, _ = row_routes if axis == "row" else layer_routes
        return exchange(axis, [state[f"to_direct_{i}"] for i in range(len(pairs))], state["to_single"])

    def messages(axis, paired, single):
        pairs, _ = row_routes if axis == "row" else layer_routes
        return {f"to_direct_{i}": VMEM(paired, F32) for i in range(len(pairs))} | {"to_single": VMEM(single, F32)}

    def column_of(r, level, k):
        return r.lists[((level - 1) * owners + r.row) * blocks + k]

    def chip_rows(z):
        return pl.ds(pl.multiple_of(z * each, each), each)

    def packed(residual):
        total = jnp.zeros((probes, size), F32)
        for level in range(levels):
            wide = jnp.concatenate([residual[level, 0], jnp.zeros((probes, size - width), F32)], axis=1)
            total = total + (pltpu.roll(wide, level * width, 1) if level else wide)
        return total

    def pack_body(r):
        copy = pltpu.make_async_copy(r.residual, r.near, r.sems.at[0])
        copy.start()
        block = pltpu.make_async_copy(r.diag_inverse.at[0, 0], r.inverse_0, r.sems.at[1])
        block.start()
        others = [
            pltpu.make_async_copy(r.diag_inverse.at[1, 0], r.inverse_1, r.sems.at[2]),
            pltpu.make_async_copy(r.lower_blocks.at[0, 0], r.lower_1, r.sems.at[3]),
        ]
        for other in others:
            other.start()
        copy.wait()
        r.packed[...] = packed(r.near)
        block.wait()
        for other in others:
            other.wait()

    def spread_body(r):
        r.other[...] = packed(r.passed)
        for name, z in outgoing(r, "layer"):
            message = getattr(r, name)
            message[r.core] = r.packed[chip_rows(z)]
            message[1 - r.core] = r.other[chip_rows(z)]

    def lists_body(r):
        for level in range(levels - 1):
            for owner in range(owners):
                for k in range(blocks):
                    r.lists[(level * owners + owner) * blocks + k] = r.listed[k, owner, level]

    def inverse(r, level):
        return r.inverse_1[...] if level == 1 else r.inverses[level, 0]

    def lower(r, level, k):
        return r.lower_1[k] if level == 1 else r.lowers[level - 1, 0, k]

    def turn_body(level):
        def body(r):
            r.turned[0] = r.inverses[level, 0].T
            for k in range(blocks):
                r.turned[1 + k] = r.lowers[level - 1, 0, k].T

        return body

    def begin_body(r):
        r.pieces[CORES * r.z + r.core] = r.packed[chip_rows(r.z)]
        r.pieces[CORES * r.z + 1 - r.core] = r.other[chip_rows(r.z)]
        for name, z in partners(r, "layer"):
            for core in range(CORES):
                r.pieces[CORES * z + core] = getattr(r, name)[core]
        answer = times(regroup_one([r.pieces[c] for c in range(columns)], width, 0), r.inverse_0[...], True)
        r.finished[r.row] = answer
        r.solved[...] = answer

    def source_body(r):
        moved = regroup([r.pieces[c] for c in range(columns)], width)
        for level in range(1, levels):
            r.source[level] = moved(level)

    def forward_body(level):
        def body(r):
            for name, owner in partners(r, "row"):
                r.finished[(level - 1) * owners + owner] = getattr(r, name)[...]
            total = r.source[level]
            for k in range(blocks):
                block = r.turned[1 + k] if level > 1 else lower(r, level, k)
                total = total - times(r.finished[column_of(r, level, k)], block, level == 1)
            answer = times(total, r.turned[0] if level > 1 else inverse(r, level), level == 1)
            r.finished[level * owners + r.row] = answer
            if level < levels - 1:
                r.solved[...] = answer
            else:
                r.accumulated[...] = jnp.zeros_like(r.accumulated)
                r.answers[...] = jnp.zeros_like(r.answers)
                backward(r, level, answer)

        return body

    def backward(r, level, source):
        answer = times(source, inverse(r, level), False)
        r.answers[level] = answer
        products = [times(answer, lower(r, level, k), False) for k in range(blocks)]
        for name, owner in outgoing(r, "row"):
            row = (level - 1) * owners + owner
            total = r.accumulated[row]
            for k in range(blocks):
                total = total + jnp.where(column_of(r, level, k) == row, products[k], 0.0)
            getattr(r, name)[...] = total
        for k in range(blocks):
            r.accumulated[column_of(r, level, k)] += products[k]

    def source_of(r, level):
        row = level * owners + r.row
        total = r.finished[row] - r.accumulated[row]
        for name, _ in partners(r, "row"):
            total = total - getattr(r, name)[...]
        return total

    def last_body(r):
        r.answers[0] = times(source_of(r, 0), r.inverse_0[...], False)
        moved = regroup([r.answers[level] for level in range(levels)], width)
        for column in range(columns):
            r.pieces[column] = moved(column)
        for name, z in outgoing(r, "layer"):
            for core in range(CORES):
                getattr(r, name)[core] = r.pieces[CORES * z + core]
        r.kept[...] = r.pieces[CORES * r.z + r.core]

    def out_body(r):
        r.whole[chip_rows(r.z)] = r.kept[...]
        for name, z in partners(r, "layer"):
            r.whole[chip_rows(z)] = getattr(r, name)[r.core]
        whole = r.whole[...]
        for level in range(levels):
            moved = pltpu.roll(whole, size - level * width, 1) if level else whole
            r.out[level, 0] = moved[:, :width]

    blocks_in = {"diag_inverse": diag_inverse, "lower_blocks": lower_blocks}
    first_blocks = {"inverse_1": VMEM((size, size), BF16), "lower_1": VMEM((blocks, size, size), BF16)}
    at_start = call(
        "pack", pack_body, {"residual": residual_in, **blocks_in},
        makes={"packed": VMEM((probes, size), F32), "inverse_0": VMEM((size, size), BF16), **first_blocks},
        scratch={"near": VMEM(residual_in.shape, F32), "sems": dma((4,))},
    )
    both = (CORES, each, size)
    spread = call(
        "spread", spread_body, {"packed": at_start["packed"], "passed": swap(residual_in)},
        makes={"other": VMEM((probes, size), F32), **messages("layer", both, both)},
    )
    arrived = exchanged("layer", spread)
    lists = call(
        "lists", lists_body, {"listed": column_lists.transpose(2, 1, 0), "after": arrived["direct_0"]},
        makes={"lists": SMEM((column_lists.size,), jnp.int32)},
    )["lists"]
    begun = call(
        "forward_0", begin_body,
        {
            "packed": at_start["packed"], "other": spread["other"], "inverse_0": at_start["inverse_0"], "lists": lists,
            **arrived,
        },
        makes={"pieces": packed_rows, "finished": all_rows, "solved": rows},
    )
    held = {1: {key: at_start[key] for key in first_blocks}}
    source = call("source", source_body, {"pieces": begun["pieces"]}, makes={"source": own_rows})["source"]
    finished, solved = begun["finished"], begun["solved"]
    to_owners = messages("row", (each, size), (each, size))
    for level in range(1, levels):
        last = level == levels - 1
        arrived = exchange("row", [solved] * len(row_routes[0]), solved)
        held.setdefault(level, {"inverses": diag_inverse, "lowers": lower_blocks})
        turned = {}
        if level > 1:
            turned = call(
                f"turn_{level}", turn_body(level), {**held[level], "after": solved},
                makes={"turned": VMEM((1 + blocks, size, size), BF16)},
            )
        state = call(
            f"forward_{level}", forward_body(level),
            {"lists": lists, **held[level], **turned, "source": source, **arrived},
            {"finished": finished},
            {"accumulated": all_rows, "answers": own_rows, **to_owners} if last else {"solved": rows},
        )
        finished, solved = state["finished"], state.get("solved")
    for level in reversed(range(1, levels - 1)):
        state = call(
            f"backward_{level}", lambda r, level=level: backward(r, level, source_of(r, level)),
            {"lists": lists, **held[level], "finished": finished, **exchanged("row", state)},
            {"accumulated": state["accumulated"], "answers": state["answers"]}, to_owners,
        )
    ended = call(
        "backward_0", last_body,
        {
            "inverse_0": at_start["inverse_0"], "finished": finished, "accumulated": state["accumulated"],
            **exchanged("row", state),
        },
        {"answers": state["answers"]},
        {"kept": rows, **messages("layer", both, both)},
        {"pieces": packed_rows},
    )
    return call(
        "out", out_body, {"kept": ended["kept"], **exchanged("layer", ended)},
        makes={"out": jax.ShapeDtypeStruct(residual_in.shape, F32)},
        scratch={"whole": VMEM((probes, size), F32)},
    )["out"]


def solution(mesh):
    placed = (
        P(None, "row", None, "col"),
        P(None, "row", None, None),
        P(None, "row", None, None, None),
        P(),
    )
    return jax.shard_map(
        shards, mesh=mesh, in_specs=placed, out_specs=P(None, "row", None, "col"), check_vma=False
    )
```

```python
import types

import jax
import jax.numpy as jnp
from jax import lax
from jax.experimental import pallas as pl
from jax.experimental.pallas import tpu as pltpu
from jax.sharding import PartitionSpec as P

VMEM = pltpu.VMEM
SMEM = pltpu.SMEM
F32 = jnp.float32
BF16 = jnp.bfloat16
CORES = 2
FAR = ("residual", "diag_inverse", "lower_blocks", "listed")


def two_parts(rows):
    high = rows.astype(BF16).astype(F32)
    return jnp.concatenate([high, rows - high], axis=0).astype(BF16)


def times(rows, block, transposed):
    contract = 1 if transposed else 0
    product = lax.dot_general(
        two_parts(rows), block, (((1,), (contract,)), ((), ())), preferred_element_type=F32
    )
    count = rows.shape[0]
    return product[:count] + product[count:]


def lane_group(shape, width):
    return lax.broadcasted_iota(jnp.int32, shape, 1) // width


def regroup(pieces, width):
    rows, size = pieces[0].shape
    groups = size // width
    stacked = jnp.concatenate(pieces, axis=0)
    rolled = [stacked if d == 0 else pltpu.roll(stacked, d * width, 1) for d in range(groups)]
    group = lane_group((rows, size), width)

    def result(b):
        total = jnp.zeros((rows, size), F32)
        for a in range(len(pieces)):
            moved = rolled[(a - b) % groups][a * rows : (a + 1) * rows]
            total = jnp.where(group == a, moved, total)
        return total

    return result


def regroup_one(pieces, width, b):
    rows, size = pieces[0].shape
    groups = size // width
    group = lane_group((rows, size), width)
    total = jnp.zeros((rows, size), F32)
    for a, piece in enumerate(pieces):
        shift = (a - b) % groups
        total = jnp.where(group == a, pltpu.roll(piece, shift * width, 1) if shift else piece, total)
    return total


def routes(count):
    order = [mask for mask in (1, 3, 2) if mask < count] + list(range(4, count))
    return [tuple(order[i : i + 2]) for i in range(0, len(order) - 1, 2)], order[-1]


def placed_in(key, array):
    space = SMEM if key == "lists" else pltpu.HBM if key in FAR else VMEM
    return pltpu.with_memory_space_constraint(array, space)


def call(name, body, reads, updates=None, makes=None, scratch=None, cost=None):
    updates, makes, scratch = updates or {}, makes or {}, scratch or {}
    ins = {**reads, **updates}
    outs = {key: VMEM(value.shape, value.dtype) for key, value in updates.items()} | makes
    in_names, out_names, scratch_names = list(ins), list(outs), list(scratch)

    def kernel(*refs):
        space = types.SimpleNamespace()
        for key, ref in zip(in_names + out_names + scratch_names, refs, strict=True):
            setattr(space, key, ref)
        column = lax.axis_index("col")
        space.row, space.z, space.core = lax.axis_index("row"), lax.div(column, CORES), lax.rem(column, CORES)
        body(space)

    def spec(key):
        if key in ("lists", "listed"):
            return pl.BlockSpec(memory_space=SMEM)
        return pl.BlockSpec(memory_space=pltpu.HBM if key in FAR else VMEM)

    results = pl.pallas_call(
        kernel,
        in_specs=[spec(key) for key in in_names],
        out_specs=[spec(key) for key in out_names],
        out_shape=[outs[key] for key in out_names],
        input_output_aliases={in_names.index(key): out_names.index(key) for key in updates},
        scratch_shapes=list(scratch.values()),
        compiler_params=pltpu.CompilerParams(vmem_limit_bytes=24 * 2**20),
        cost_estimate=cost,
        name=name,
    )(*[placed_in(key, value) for key, value in ins.items()])
    return dict(zip(out_names, results, strict=True))


def shards(residual_in, diag_inverse, lower_blocks, column_lists):
    levels, _, probes, width = residual_in.shape
    size = diag_inverse.shape[-1]
    owners, columns = lax.axis_size("row"), lax.axis_size("col")
    layers = columns // CORES
    each = probes // layers
    blocks = column_lists.shape[2]
    rows = VMEM((each, size), F32)
    own_rows = VMEM((levels, each, size), F32)
    all_rows = VMEM((levels * owners, each, size), F32)
    packed_rows = VMEM((columns, each, size), F32)
    row_routes, layer_routes = routes(owners), routes(layers)
    dma = pltpu.SemaphoreType.DMA

    def swap(array):
        return lax.ppermute(array, "col", [(c, c ^ 1) for c in range(columns)])

    def exchange(axis, paired, single):
        pairs, last = row_routes if axis == "row" else layer_routes

        def send(array, masks):
            steps = []
            for row in range(owners):
                for column in range(columns):
                    mask = masks[column % CORES]
                    to = (row ^ mask, column) if axis == "row" else (row, column ^ (CORES * mask))
                    steps.append((row * columns + column, to[0] * columns + to[1]))
            return lax.ppermute(array, ("row", "col"), steps)

        got = {"single": send(single, (last, last))}
        for i, masks in enumerate(pairs):
            got[f"direct_{i}"] = send(paired[i], masks)
        for i in range(len(pairs)):
            got[f"passed_{i}"] = swap(got[f"direct_{i}"])
        return got

    def partners(r, axis):
        pairs, last = row_routes if axis == "row" else layer_routes
        here = r.row if axis == "row" else r.z
        found = []
        for i, (one, other) in enumerate(pairs):
            found.append((f"direct_{i}", here ^ jnp.where(r.core == 0, one, other)))
            found.append((f"passed_{i}", here ^ jnp.where(r.core == 0, other, one)))
        return found + [("single", here ^ last)]

    def outgoing(r, axis):
        return [(f"to_{name}", to) for name, to in partners(r, axis) if not name.startswith("passed")]

    def exchanged(axis, state):
        pairs, _ = row_routes if axis == "row" else layer_routes
        return exchange(axis, [state[f"to_direct_{i}"] for i in range(len(pairs))], state["to_single"])

    def messages(axis, paired, single):
        pairs, _ = row_routes if axis == "row" else layer_routes
        return {f"to_direct_{i}": VMEM(paired, F32) for i in range(len(pairs))} | {"to_single": VMEM(single, F32)}

    def column_of(r, level, k):
        return r.lists[((level - 1) * owners + r.row) * blocks + k]

    def chip_rows(z):
        return pl.ds(pl.multiple_of(z * each, each), each)

    def packed(residual):
        total = jnp.zeros((probes, size), F32)
        for level in range(levels):
            wide = jnp.concatenate([residual[level, 0], jnp.zeros((probes, size - width), F32)], axis=1)
            total = total + (pltpu.roll(wide, level * width, 1) if level else wide)
        return total

    def pack_body(r):
        copy = pltpu.make_async_copy(r.residual, r.near, r.sems.at[0])
        copy.start()
        block = pltpu.make_async_copy(r.diag_inverse.at[0, 0], r.inverse_0, r.sems.at[1])
        block.start()
        others = [
            pltpu.make_async_copy(r.diag_inverse.at[1, 0], r.inverse_1, r.sems.at[2]),
            pltpu.make_async_copy(r.lower_blocks.at[0, 0], r.lower_1, r.sems.at[3]),
        ]
        for other in others:
            other.start()
        copy.wait()
        r.packed[...] = packed(r.near)
        block.wait()
        for other in others:
            other.wait()

    def spread_body(r):
        r.other[...] = packed(r.passed)
        for name, z in outgoing(r, "layer"):
            message = getattr(r, name)
            message[r.core] = r.packed[chip_rows(z)]
            message[1 - r.core] = r.other[chip_rows(z)]

    def lists_body(r):
        for level in range(levels - 1):
            for owner in range(owners):
                for k in range(blocks):
                    r.lists[(level * owners + owner) * blocks + k] = r.listed[k, owner, level]

    def inverse(r, level):
        return r.inverse_1[...] if level == 1 else r.inverses[level, 0]

    def lower(r, level, k):
        return r.lower_1[k] if level == 1 else r.lowers[level - 1, 0, k]

    def turn_body(level):
        def body(r):
            r.turned[0] = inverse(r, level).T
            for k in range(blocks):
                r.turned[1 + k] = lower(r, level, k).T

        return body

    def begin_body(r):
        r.pieces[CORES * r.z + r.core] = r.packed[chip_rows(r.z)]
        r.pieces[CORES * r.z + 1 - r.core] = r.other[chip_rows(r.z)]
        for name, z in partners(r, "layer"):
            for core in range(CORES):
                r.pieces[CORES * z + core] = getattr(r, name)[core]
        answer = times(regroup_one([r.pieces[c] for c in range(columns)], width, 0), r.inverse_0[...], True)
        r.finished[r.row] = answer
        r.solved[...] = answer

    def source_body(r):
        moved = regroup([r.pieces[c] for c in range(columns)], width)
        for level in range(1, levels):
            r.source[level] = moved(level)

    def forward_body(level):
        def body(r):
            for name, owner in partners(r, "row"):
                r.finished[(level - 1) * owners + owner] = getattr(r, name)[...]
            total = r.source[level]
            for k in range(blocks):
                total = total - times(r.finished[column_of(r, level, k)], r.turned[1 + k], False)
            answer = times(total, r.turned[0], False)
            r.finished[level * owners + r.row] = answer
            if level < levels - 1:
                r.solved[...] = answer
            else:
                r.accumulated[...] = jnp.zeros_like(r.accumulated)
                r.answers[...] = jnp.zeros_like(r.answers)
                backward(r, level, answer)

        return body

    def backward(r, level, source):
        answer = times(source, inverse(r, level), False)
        r.answers[level] = answer
        products = [times(answer, lower(r, level, k), False) for k in range(blocks)]
        for name, owner in outgoing(r, "row"):
            row = (level - 1) * owners + owner
            total = r.accumulated[row]
            for k in range(blocks):
                total = total + jnp.where(column_of(r, level, k) == row, products[k], 0.0)
            getattr(r, name)[...] = total
        for k in range(blocks):
            r.accumulated[column_of(r, level, k)] += products[k]

    def source_of(r, level):
        row = level * owners + r.row
        total = r.finished[row] - r.accumulated[row]
        for name, _ in partners(r, "row"):
            total = total - getattr(r, name)[...]
        return total

    def gather_body(r):
        moved = regroup([jnp.zeros((each, size), F32)] + [r.answers[level] for level in range(1, levels)], width)
        for column in range(columns):
            r.pieces[column] = moved(column)

    def last_body(r):
        answer = times(source_of(r, 0), r.inverse_0[...], False)
        first = lane_group((each, size), width) == 0
        for column in range(columns):
            moved = pltpu.roll(answer, size - column * width, 1) if column else answer
            r.pieces[column] = jnp.where(first, moved, r.pieces[column])
        for name, z in outgoing(r, "layer"):
            for core in range(CORES):
                getattr(r, name)[core] = r.pieces[CORES * z + core]
        r.kept[...] = r.pieces[CORES * r.z + r.core]

    def out_body(r):
        r.whole[chip_rows(r.z)] = r.kept[...]
        for name, z in partners(r, "layer"):
            r.whole[chip_rows(z)] = getattr(r, name)[r.core]
        whole = r.whole[...]
        for level in range(levels):
            moved = pltpu.roll(whole, size - level * width, 1) if level else whole
            r.out[level, 0] = moved[:, :width]

    blocks_in = {"diag_inverse": diag_inverse, "lower_blocks": lower_blocks}
    first_blocks = {"inverse_1": VMEM((size, size), BF16), "lower_1": VMEM((blocks, size, size), BF16)}
    at_start = call(
        "pack", pack_body, {"residual": residual_in, **blocks_in},
        makes={"packed": VMEM((probes, size), F32), "inverse_0": VMEM((size, size), BF16), **first_blocks},
        scratch={"near": VMEM(residual_in.shape, F32), "sems": dma((4,))},
    )
    both = (CORES, each, size)
    spread = call(
        "spread", spread_body, {"packed": at_start["packed"], "passed": swap(residual_in)},
        makes={"other": VMEM((probes, size), F32), **messages("layer", both, both)},
    )
    arrived = exchanged("layer", spread)
    lists = call(
        "lists", lists_body, {"listed": column_lists.transpose(2, 1, 0), "after": arrived["direct_0"]},
        makes={"lists": SMEM((column_lists.size,), jnp.int32)},
    )["lists"]
    begun = call(
        "forward_0", begin_body,
        {
            "packed": at_start["packed"], "other": spread["other"], "inverse_0": at_start["inverse_0"], "lists": lists,
            **arrived,
        },
        makes={"pieces": packed_rows, "finished": all_rows, "solved": rows},
    )
    held = {1: {key: at_start[key] for key in first_blocks}}
    source = call("source", source_body, {"pieces": begun["pieces"]}, makes={"source": own_rows})["source"]
    finished, solved = begun["finished"], begun["solved"]
    to_owners = messages("row", (each, size), (each, size))
    for level in range(1, levels):
        last = level == levels - 1
        arrived = exchange("row", [solved] * len(row_routes[0]), solved)
        held.setdefault(level, {"inverses": diag_inverse, "lowers": lower_blocks})
        turned = call(
            f"turn_{level}", turn_body(level), {**held[level], "after": solved},
            makes={"turned": VMEM((1 + blocks, size, size), BF16)},
        )
        state = call(
            f"forward_{level}", forward_body(level),
            {"lists": lists, **(held[level] if last else {}), **turned, "source": source, **arrived},
            {"finished": finished},
            {"accumulated": all_rows, "answers": own_rows, **to_owners} if last else {"solved": rows},
        )
        finished, solved = state["finished"], state.get("solved")
    for level in reversed(range(1, levels - 1)):
        state = call(
            f"backward_{level}", lambda r, level=level: backward(r, level, source_of(r, level)),
            {"lists": lists, **held[level], "finished": finished, **exchanged("row", state)},
            {"accumulated": state["accumulated"], "answers": state["answers"]}, to_owners,
        )
    arrived = exchanged("row", state)
    pieces = call("gather", gather_body, {"answers": state["answers"]}, makes={"pieces": packed_rows})["pieces"]
    ended = call(
        "backward_0", last_body,
        {
            "inverse_0": at_start["inverse_0"], "finished": finished, "accumulated": state["accumulated"], **arrived,
        },
        {"pieces": pieces},
        {"kept": rows, **messages("layer", both, both)},
    )
    return call(
        "out", out_body, {"kept": ended["kept"], **exchanged("layer", ended)},
        makes={"out": jax.ShapeDtypeStruct(residual_in.shape, F32)},
        scratch={"whole": VMEM((probes, size), F32)},
    )["out"]


def solution(mesh):
    placed = (
        P(None, "row", None, "col"),
        P(None, "row", None, None),
        P(None, "row", None, None, None),
        P(),
    )
    return jax.shard_map(
        shards, mesh=mesh, in_specs=placed, out_specs=P(None, "row", None, "col"), check_vma=False
    )
```

```python
import types

import jax
import jax.numpy as jnp
from jax import lax
from jax.experimental import pallas as pl
from jax.experimental.pallas import tpu as pltpu
from jax.sharding import PartitionSpec as P

VMEM = pltpu.VMEM
SMEM = pltpu.SMEM
F32 = jnp.float32
BF16 = jnp.bfloat16
CORES = 2
FAR = ("residual", "diag_inverse", "lower_blocks", "listed")


def two_parts(rows):
    high = rows.astype(BF16).astype(F32)
    return jnp.concatenate([high, rows - high], axis=0).astype(BF16)


def times(rows, block, transposed):
    contract = 1 if transposed else 0
    product = lax.dot_general(
        two_parts(rows), block, (((1,), (contract,)), ((), ())), preferred_element_type=F32
    )
    count = rows.shape[0]
    return product[:count] + product[count:]


def lane_group(shape, width):
    return lax.broadcasted_iota(jnp.int32, shape, 1) // width


def regroup(pieces, width):
    rows, size = pieces[0].shape
    groups = size // width
    stacked = jnp.concatenate(pieces, axis=0)
    rolled = [stacked if d == 0 else pltpu.roll(stacked, d * width, 1) for d in range(groups)]
    group = lane_group((rows, size), width)

    def result(b):
        total = jnp.zeros((rows, size), F32)
        for a in range(len(pieces)):
            moved = rolled[(a - b) % groups][a * rows : (a + 1) * rows]
            total = jnp.where(group == a, moved, total)
        return total

    return result


def regroup_one(pieces, width, b):
    rows, size = pieces[0].shape
    groups = size // width
    group = lane_group((rows, size), width)
    total = jnp.zeros((rows, size), F32)
    for a, piece in enumerate(pieces):
        shift = (a - b) % groups
        total = jnp.where(group == a, pltpu.roll(piece, shift * width, 1) if shift else piece, total)
    return total


def routes(count, first):
    order = [mask for mask in first if mask < count] + list(range(4, count))
    return [tuple(order[i : i + 2]) for i in range(0, len(order) - 1, 2)], order[-1]


def placed_in(key, array):
    space = SMEM if key == "lists" else pltpu.HBM if key in FAR else VMEM
    return pltpu.with_memory_space_constraint(array, space)


def call(name, body, reads, updates=None, makes=None, scratch=None, cost=None):
    updates, makes, scratch = updates or {}, makes or {}, scratch or {}
    ins = {**reads, **updates}
    outs = {key: VMEM(value.shape, value.dtype) for key, value in updates.items()} | makes
    in_names, out_names, scratch_names = list(ins), list(outs), list(scratch)

    def kernel(*refs):
        space = types.SimpleNamespace()
        for key, ref in zip(in_names + out_names + scratch_names, refs, strict=True):
            setattr(space, key, ref)
        column = lax.axis_index("col")
        space.row, space.z, space.core = lax.axis_index("row"), lax.div(column, CORES), lax.rem(column, CORES)
        body(space)

    def spec(key):
        if key in ("lists", "listed"):
            return pl.BlockSpec(memory_space=SMEM)
        return pl.BlockSpec(memory_space=pltpu.HBM if key in FAR else VMEM)

    results = pl.pallas_call(
        kernel,
        in_specs=[spec(key) for key in in_names],
        out_specs=[spec(key) for key in out_names],
        out_shape=[outs[key] for key in out_names],
        input_output_aliases={in_names.index(key): out_names.index(key) for key in updates},
        scratch_shapes=list(scratch.values()),
        compiler_params=pltpu.CompilerParams(vmem_limit_bytes=24 * 2**20),
        cost_estimate=cost,
        name=name,
    )(*[placed_in(key, value) for key, value in ins.items()])
    return dict(zip(out_names, results, strict=True))


def shards(residual_in, diag_inverse, lower_blocks, column_lists):
    levels, _, probes, width = residual_in.shape
    size = diag_inverse.shape[-1]
    owners, columns = lax.axis_size("row"), lax.axis_size("col")
    layers = columns // CORES
    each = probes // layers
    blocks = column_lists.shape[2]
    rows = VMEM((each, size), F32)
    own_rows = VMEM((levels, each, size), F32)
    all_rows = VMEM((levels * owners, each, size), F32)
    packed_rows = VMEM((columns, each, size), F32)
    row_routes, layer_routes = routes(owners, (1, 3, 2)), routes(layers, (2, 3, 1))
    dma = pltpu.SemaphoreType.DMA

    def swap(array):
        return lax.ppermute(array, "col", [(c, c ^ 1) for c in range(columns)])

    def exchange(axis, paired, single):
        pairs, last = row_routes if axis == "row" else layer_routes

        def send(array, masks):
            steps = []
            for row in range(owners):
                for column in range(columns):
                    mask = masks[column % CORES]
                    to = (row ^ mask, column) if axis == "row" else (row, column ^ (CORES * mask))
                    steps.append((row * columns + column, to[0] * columns + to[1]))
            return lax.ppermute(array, ("row", "col"), steps)

        got = {"single": send(single, (last, last))}
        for i, masks in enumerate(pairs):
            got[f"direct_{i}"] = send(paired[i], masks)
        for i in range(len(pairs)):
            got[f"passed_{i}"] = swap(got[f"direct_{i}"])
        return got

    def partners(r, axis):
        pairs, last = row_routes if axis == "row" else layer_routes
        here = r.row if axis == "row" else r.z
        found = []
        for i, (one, other) in enumerate(pairs):
            found.append((f"direct_{i}", here ^ jnp.where(r.core == 0, one, other)))
            found.append((f"passed_{i}", here ^ jnp.where(r.core == 0, other, one)))
        return found + [("single", here ^ last)]

    def outgoing(r, axis):
        return [(f"to_{name}", to) for name, to in partners(r, axis) if not name.startswith("passed")]

    def exchanged(axis, state):
        pairs, _ = row_routes if axis == "row" else layer_routes
        return exchange(axis, [state[f"to_direct_{i}"] for i in range(len(pairs))], state["to_single"])

    def messages(axis, paired, single):
        pairs, _ = row_routes if axis == "row" else layer_routes
        return {f"to_direct_{i}": VMEM(paired, F32) for i in range(len(pairs))} | {"to_single": VMEM(single, F32)}

    def column_of(r, level, k):
        return r.lists[((level - 1) * owners + r.row) * blocks + k]

    def chip_rows(z):
        return pl.ds(pl.multiple_of(z * each, each), each)

    def packed(residual):
        total = jnp.zeros((probes, size), F32)
        for level in range(levels):
            wide = jnp.concatenate([residual[level, 0], jnp.zeros((probes, size - width), F32)], axis=1)
            total = total + (pltpu.roll(wide, level * width, 1) if level else wide)
        return total

    def pack_body(r):
        copy = pltpu.make_async_copy(r.residual, r.near, r.sems.at[0])
        copy.start()
        block = pltpu.make_async_copy(r.diag_inverse.at[0, 0], r.inverse_0, r.sems.at[1])
        block.start()
        others = [
            pltpu.make_async_copy(r.diag_inverse.at[1, 0], r.inverse_1, r.sems.at[2]),
            pltpu.make_async_copy(r.lower_blocks.at[0, 0], r.lower_1, r.sems.at[3]),
        ]
        for other in others:
            other.start()
        copy.wait()
        r.packed[...] = packed(r.near)
        block.wait()
        for other in others:
            other.wait()

    def spread_body(r):
        r.other[...] = packed(r.passed)
        for name, z in outgoing(r, "layer"):
            message = getattr(r, name)
            message[r.core] = r.packed[chip_rows(z)]
            message[1 - r.core] = r.other[chip_rows(z)]

    def lists_body(r):
        for level in range(levels - 1):
            for owner in range(owners):
                for k in range(blocks):
                    r.lists[(level * owners + owner) * blocks + k] = r.listed[k, owner, level]

    def inverse(r, level):
        return r.inverse_1[...] if level == 1 else r.inverses[level, 0]

    def lower(r, level, k):
        return r.lower_1[k] if level == 1 else r.lowers[level - 1, 0, k]

    def turn_body(level):
        def body(r):
            r.turned[0] = inverse(r, level).T
            for k in range(blocks):
                r.turned[1 + k] = lower(r, level, k).T

        return body

    def begin_body(r):
        r.pieces[CORES * r.z + r.core] = r.packed[chip_rows(r.z)]
        r.pieces[CORES * r.z + 1 - r.core] = r.other[chip_rows(r.z)]
        for name, z in partners(r, "layer"):
            for core in range(CORES):
                r.pieces[CORES * z + core] = getattr(r, name)[core]
        answer = times(regroup_one([r.pieces[c] for c in range(columns)], width, 0), r.inverse_0[...], True)
        r.finished[r.row] = answer
        r.solved[...] = answer

    def source_body(r):
        moved = regroup([r.pieces[c] for c in range(columns)], width)
        for level in range(1, levels):
            r.source[level] = moved(level)

    def forward_body(level):
        def body(r):
            for name, owner in partners(r, "row"):
                r.finished[(level - 1) * owners + owner] = getattr(r, name)[...]
            total = r.source[level]
            for k in range(blocks):
                total = total - times(r.finished[column_of(r, level, k)], r.turned[1 + k], False)
            answer = times(total, r.turned[0], False)
            r.finished[level * owners + r.row] = answer
            if level < levels - 1:
                r.solved[...] = answer
            else:
                r.accumulated[...] = jnp.zeros_like(r.accumulated)
                r.answers[...] = jnp.zeros_like(r.answers)
                backward(r, level, answer)

        return body

    def backward(r, level, source):
        answer = times(source, inverse(r, level), False)
        r.answers[level] = answer
        products = [times(answer, lower(r, level, k), False) for k in range(blocks)]
        for name, owner in outgoing(r, "row"):
            row = (level - 1) * owners + owner
            total = r.accumulated[row]
            for k in range(blocks):
                total = total + jnp.where(column_of(r, level, k) == row, products[k], 0.0)
            getattr(r, name)[...] = total
        for k in range(blocks):
            r.accumulated[column_of(r, level, k)] += products[k]

    def source_of(r, level):
        row = level * owners + r.row
        total = r.finished[row] - r.accumulated[row]
        for name, _ in partners(r, "row"):
            total = total - getattr(r, name)[...]
        return total

    def gather_body(r):
        moved = regroup([jnp.zeros((each, size), F32)] + [r.answers[level] for level in range(1, levels)], width)
        for column in range(columns):
            r.pieces[column] = moved(column)

    def last_body(r):
        answer = times(source_of(r, 0), r.inverse_0[...], False)
        first = lane_group((each, size), width) == 0
        for column in range(columns):
            moved = pltpu.roll(answer, size - column * width, 1) if column else answer
            r.pieces[column] = jnp.where(first, moved, r.pieces[column])
        for name, z in outgoing(r, "layer"):
            for core in range(CORES):
                getattr(r, name)[core] = r.pieces[CORES * z + core]
        r.kept[...] = r.pieces[CORES * r.z + r.core]

    def out_body(r):
        r.whole[chip_rows(r.z)] = r.kept[...]
        for name, z in partners(r, "layer"):
            r.whole[chip_rows(z)] = getattr(r, name)[r.core]
        whole = r.whole[...]
        for level in range(levels):
            moved = pltpu.roll(whole, size - level * width, 1) if level else whole
            r.out[level, 0] = moved[:, :width]

    blocks_in = {"diag_inverse": diag_inverse, "lower_blocks": lower_blocks}
    first_blocks = {"inverse_1": VMEM((size, size), BF16), "lower_1": VMEM((blocks, size, size), BF16)}
    at_start = call(
        "pack", pack_body, {"residual": residual_in, **blocks_in},
        makes={"packed": VMEM((probes, size), F32), "inverse_0": VMEM((size, size), BF16), **first_blocks},
        scratch={"near": VMEM(residual_in.shape, F32), "sems": dma((4,))},
    )
    both = (CORES, each, size)
    spread = call(
        "spread", spread_body, {"packed": at_start["packed"], "passed": swap(residual_in)},
        makes={"other": VMEM((probes, size), F32), **messages("layer", both, both)},
    )
    arrived = exchanged("layer", spread)
    lists = call(
        "lists", lists_body, {"listed": column_lists.transpose(2, 1, 0), "after": arrived["direct_0"]},
        makes={"lists": SMEM((column_lists.size,), jnp.int32)},
    )["lists"]
    begun = call(
        "forward_0", begin_body,
        {
            "packed": at_start["packed"], "other": spread["other"], "inverse_0": at_start["inverse_0"], "lists": lists,
            **arrived,
        },
        makes={"pieces": packed_rows, "finished": all_rows, "solved": rows},
    )
    held = {1: {key: at_start[key] for key in first_blocks}}
    source = call("source", source_body, {"pieces": begun["pieces"]}, makes={"source": own_rows})["source"]
    finished, solved = begun["finished"], begun["solved"]
    to_owners = messages("row", (each, size), (each, size))
    for level in range(1, levels):
        last = level == levels - 1
        arrived = exchange("row", [solved] * len(row_routes[0]), solved)
        held.setdefault(level, {"inverses": diag_inverse, "lowers": lower_blocks})
        turned = call(
            f"turn_{level}", turn_body(level), {**held[level], "after": solved},
            makes={"turned": VMEM((1 + blocks, size, size), BF16)},
        )
        state = call(
            f"forward_{level}", forward_body(level),
            {"lists": lists, **(held[level] if last else {}), **turned, "source": source, **arrived},
            {"finished": finished},
            {"accumulated": all_rows, "answers": own_rows, **to_owners} if last else {"solved": rows},
        )
        finished, solved = state["finished"], state.get("solved")
    for level in reversed(range(1, levels - 1)):
        state = call(
            f"backward_{level}", lambda r, level=level: backward(r, level, source_of(r, level)),
            {"lists": lists, **held[level], "finished": finished, **exchanged("row", state)},
            {"accumulated": state["accumulated"], "answers": state["answers"]}, to_owners,
        )
    arrived = exchanged("row", state)
    pieces = call("gather", gather_body, {"answers": state["answers"]}, makes={"pieces": packed_rows})["pieces"]
    ended = call(
        "backward_0", last_body,
        {
            "inverse_0": at_start["inverse_0"], "finished": finished, "accumulated": state["accumulated"], **arrived,
        },
        {"pieces": pieces},
        {"kept": rows, **messages("layer", both, both)},
    )
    return call(
        "out", out_body, {"kept": ended["kept"], **exchanged("layer", ended)},
        makes={"out": jax.ShapeDtypeStruct(residual_in.shape, F32)},
        scratch={"whole": VMEM((probes, size), F32)},
    )["out"]


def solution(mesh):
    placed = (
        P(None, "row", None, "col"),
        P(None, "row", None, None),
        P(None, "row", None, None, None),
        P(),
    )
    return jax.shard_map(
        shards, mesh=mesh, in_specs=placed, out_specs=P(None, "row", None, "col"), check_vma=False
    )
```

```python
import types

import jax
import jax.numpy as jnp
from jax import lax
from jax.experimental import pallas as pl
from jax.experimental.pallas import tpu as pltpu
from jax.sharding import PartitionSpec as P

VMEM = pltpu.VMEM
SMEM = pltpu.SMEM
F32 = jnp.float32
BF16 = jnp.bfloat16
CORES = 2
FAR = ("residual", "diag_inverse", "lower_blocks", "listed")


def two_parts(rows):
    high = rows.astype(BF16).astype(F32)
    return jnp.concatenate([high, rows - high], axis=0).astype(BF16)


def times(rows, block, transposed):
    contract = 1 if transposed else 0
    product = lax.dot_general(
        two_parts(rows), block, (((1,), (contract,)), ((), ())), preferred_element_type=F32
    )
    count = rows.shape[0]
    return product[:count] + product[count:]


def lane_group(shape, width):
    return lax.broadcasted_iota(jnp.int32, shape, 1) // width


def regroup(pieces, width):
    rows, size = pieces[0].shape
    groups = size // width
    stacked = jnp.concatenate(pieces, axis=0)
    rolled = [stacked if d == 0 else pltpu.roll(stacked, d * width, 1) for d in range(groups)]
    group = lane_group((rows, size), width)

    def result(b):
        total = jnp.zeros((rows, size), F32)
        for a in range(len(pieces)):
            moved = rolled[(a - b) % groups][a * rows : (a + 1) * rows]
            total = jnp.where(group == a, moved, total)
        return total

    return result


def regroup_one(pieces, width, b):
    rows, size = pieces[0].shape
    groups = size // width
    group = lane_group((rows, size), width)
    total = jnp.zeros((rows, size), F32)
    for a, piece in enumerate(pieces):
        shift = (a - b) % groups
        total = jnp.where(group == a, pltpu.roll(piece, shift * width, 1) if shift else piece, total)
    return total


def routes(count, first):
    order = [mask for mask in first if mask < count] + list(range(4, count))
    return [tuple(order[i : i + 2]) for i in range(0, len(order) - 1, 2)], order[-1]


def placed_in(key, array):
    space = SMEM if key == "lists" else pltpu.HBM if key in FAR else VMEM
    return pltpu.with_memory_space_constraint(array, space)


def call(name, body, reads, updates=None, makes=None, scratch=None, cost=None):
    updates, makes, scratch = updates or {}, makes or {}, scratch or {}
    ins = {**reads, **updates}
    outs = {key: VMEM(value.shape, value.dtype) for key, value in updates.items()} | makes
    in_names, out_names, scratch_names = list(ins), list(outs), list(scratch)

    def kernel(*refs):
        space = types.SimpleNamespace()
        for key, ref in zip(in_names + out_names + scratch_names, refs, strict=True):
            setattr(space, key, ref)
        column = lax.axis_index("col")
        space.row, space.z, space.core = lax.axis_index("row"), lax.div(column, CORES), lax.rem(column, CORES)
        body(space)

    def spec(key):
        if key in ("lists", "listed"):
            return pl.BlockSpec(memory_space=SMEM)
        return pl.BlockSpec(memory_space=pltpu.HBM if key in FAR else VMEM)

    results = pl.pallas_call(
        kernel,
        in_specs=[spec(key) for key in in_names],
        out_specs=[spec(key) for key in out_names],
        out_shape=[outs[key] for key in out_names],
        input_output_aliases={in_names.index(key): out_names.index(key) for key in updates},
        scratch_shapes=list(scratch.values()),
        compiler_params=pltpu.CompilerParams(vmem_limit_bytes=24 * 2**20),
        cost_estimate=cost,
        name=name,
    )(*[placed_in(key, value) for key, value in ins.items()])
    return dict(zip(out_names, results, strict=True))


def shards(residual_in, diag_inverse, lower_blocks, column_lists):
    levels, _, probes, width = residual_in.shape
    size = diag_inverse.shape[-1]
    owners, columns = lax.axis_size("row"), lax.axis_size("col")
    layers = columns // CORES
    each = probes // layers
    blocks = column_lists.shape[2]
    rows = VMEM((each, size), F32)
    own_rows = VMEM((levels, each, size), F32)
    all_rows = VMEM((levels * owners, each, size), F32)
    packed_rows = VMEM((columns, each, size), F32)
    row_routes, layer_routes = routes(owners, (2, 3, 1)), routes(layers, (2, 3, 1))
    dma = pltpu.SemaphoreType.DMA

    def swap(array):
        return lax.ppermute(array, "col", [(c, c ^ 1) for c in range(columns)])

    def exchange(axis, paired, single):
        pairs, last = row_routes if axis == "row" else layer_routes

        def send(array, masks):
            steps = []
            for row in range(owners):
                for column in range(columns):
                    mask = masks[column % CORES]
                    to = (row ^ mask, column) if axis == "row" else (row, column ^ (CORES * mask))
                    steps.append((row * columns + column, to[0] * columns + to[1]))
            return lax.ppermute(array, ("row", "col"), steps)

        got = {"single": send(single, (last, last))}
        for i, masks in enumerate(pairs):
            got[f"direct_{i}"] = send(paired[i], masks)
        for i in range(len(pairs)):
            got[f"passed_{i}"] = swap(got[f"direct_{i}"])
        return got

    def partners(r, axis):
        pairs, last = row_routes if axis == "row" else layer_routes
        here = r.row if axis == "row" else r.z
        found = []
        for i, (one, other) in enumerate(pairs):
            found.append((f"direct_{i}", here ^ jnp.where(r.core == 0, one, other)))
            found.append((f"passed_{i}", here ^ jnp.where(r.core == 0, other, one)))
        return found + [("single", here ^ last)]

    def outgoing(r, axis):
        return [(f"to_{name}", to) for name, to in partners(r, axis) if not name.startswith("passed")]

    def exchanged(axis, state):
        pairs, _ = row_routes if axis == "row" else layer_routes
        return exchange(axis, [state[f"to_direct_{i}"] for i in range(len(pairs))], state["to_single"])

    def messages(axis, paired, single):
        pairs, _ = row_routes if axis == "row" else layer_routes
        return {f"to_direct_{i}": VMEM(paired, F32) for i in range(len(pairs))} | {"to_single": VMEM(single, F32)}

    def column_of(r, level, k):
        return r.lists[((level - 1) * owners + r.row) * blocks + k]

    def chip_rows(z):
        return pl.ds(pl.multiple_of(z * each, each), each)

    def packed(residual):
        total = jnp.zeros((probes, size), F32)
        for level in range(levels):
            wide = jnp.concatenate([residual[level, 0], jnp.zeros((probes, size - width), F32)], axis=1)
            total = total + (pltpu.roll(wide, level * width, 1) if level else wide)
        return total

    def pack_body(r):
        copy = pltpu.make_async_copy(r.residual, r.near, r.sems.at[0])
        copy.start()
        block = pltpu.make_async_copy(r.diag_inverse.at[0, 0], r.inverse_0, r.sems.at[1])
        block.start()
        others = [
            pltpu.make_async_copy(r.diag_inverse.at[1, 0], r.inverse_1, r.sems.at[2]),
            pltpu.make_async_copy(r.lower_blocks.at[0, 0], r.lower_1, r.sems.at[3]),
        ]
        for other in others:
            other.start()
        copy.wait()
        r.packed[...] = packed(r.near)
        block.wait()
        for other in others:
            other.wait()

    def spread_body(r):
        r.other[...] = packed(r.passed)
        for name, z in outgoing(r, "layer"):
            message = getattr(r, name)
            message[r.core] = r.packed[chip_rows(z)]
            message[1 - r.core] = r.other[chip_rows(z)]

    def lists_body(r):
        for level in range(levels - 1):
            for owner in range(owners):
                for k in range(blocks):
                    r.lists[(level * owners + owner) * blocks + k] = r.listed[k, owner, level]

    def inverse(r, level):
        return r.inverse_1[...] if level == 1 else r.inverses[level, 0]

    def lower(r, level, k):
        return r.lower_1[k] if level == 1 else r.lowers[level - 1, 0, k]

    def turn_body(level):
        def body(r):
            r.turned[0] = inverse(r, level).T
            for k in range(blocks):
                r.turned[1 + k] = lower(r, level, k).T

        return body

    def begin_body(r):
        r.pieces[CORES * r.z + r.core] = r.packed[chip_rows(r.z)]
        r.pieces[CORES * r.z + 1 - r.core] = r.other[chip_rows(r.z)]
        for name, z in partners(r, "layer"):
            for core in range(CORES):
                r.pieces[CORES * z + core] = getattr(r, name)[core]
        answer = times(regroup_one([r.pieces[c] for c in range(columns)], width, 0), r.inverse_0[...], True)
        r.finished[r.row] = answer
        r.solved[...] = answer

    def source_body(r):
        moved = regroup([r.pieces[c] for c in range(columns)], width)
        for level in range(1, levels):
            r.source[level] = moved(level)

    def forward_body(level):
        def body(r):
            for name, owner in partners(r, "row"):
                r.finished[(level - 1) * owners + owner] = getattr(r, name)[...]
            total = r.source[level]
            for k in range(blocks):
                total = total - times(r.finished[column_of(r, level, k)], r.turned[1 + k], False)
            answer = times(total, r.turned[0], False)
            r.finished[level * owners + r.row] = answer
            if level < levels - 1:
                r.solved[...] = answer
            else:
                r.accumulated[...] = jnp.zeros_like(r.accumulated)
                r.answers[...] = jnp.zeros_like(r.answers)
                backward(r, level, answer)

        return body

    def backward(r, level, source):
        answer = times(source, inverse(r, level), False)
        r.answers[level] = answer
        products = [times(answer, lower(r, level, k), False) for k in range(blocks)]
        for name, owner in outgoing(r, "row"):
            row = (level - 1) * owners + owner
            total = r.accumulated[row]
            for k in range(blocks):
                total = total + jnp.where(column_of(r, level, k) == row, products[k], 0.0)
            getattr(r, name)[...] = total
        for k in range(blocks):
            r.accumulated[column_of(r, level, k)] += products[k]

    def source_of(r, level):
        row = level * owners + r.row
        total = r.finished[row] - r.accumulated[row]
        for name, _ in partners(r, "row"):
            total = total - getattr(r, name)[...]
        return total

    def gather_body(r):
        moved = regroup([jnp.zeros((each, size), F32)] + [r.answers[level] for level in range(1, levels)], width)
        for column in range(columns):
            r.pieces[column] = moved(column)

    def last_body(r):
        answer = times(source_of(r, 0), r.inverse_0[...], False)
        first = lane_group((each, size), width) == 0
        for column in range(columns):
            moved = pltpu.roll(answer, size - column * width, 1) if column else answer
            r.pieces[column] = jnp.where(first, moved, r.pieces[column])
        for name, z in outgoing(r, "layer"):
            for core in range(CORES):
                getattr(r, name)[core] = r.pieces[CORES * z + core]
        r.kept[...] = r.pieces[CORES * r.z + r.core]

    def out_body(r):
        r.whole[chip_rows(r.z)] = r.kept[...]
        for name, z in partners(r, "layer"):
            r.whole[chip_rows(z)] = getattr(r, name)[r.core]
        whole = r.whole[...]
        for level in range(levels):
            moved = pltpu.roll(whole, size - level * width, 1) if level else whole
            r.out[level, 0] = moved[:, :width]

    blocks_in = {"diag_inverse": diag_inverse, "lower_blocks": lower_blocks}
    first_blocks = {"inverse_1": VMEM((size, size), BF16), "lower_1": VMEM((blocks, size, size), BF16)}
    at_start = call(
        "pack", pack_body, {"residual": residual_in, **blocks_in},
        makes={"packed": VMEM((probes, size), F32), "inverse_0": VMEM((size, size), BF16), **first_blocks},
        scratch={"near": VMEM(residual_in.shape, F32), "sems": dma((4,))},
    )
    both = (CORES, each, size)
    spread = call(
        "spread", spread_body, {"packed": at_start["packed"], "passed": swap(residual_in)},
        makes={"other": VMEM((probes, size), F32), **messages("layer", both, both)},
    )
    arrived = exchanged("layer", spread)
    lists = call(
        "lists", lists_body, {"listed": column_lists.transpose(2, 1, 0), "after": arrived["direct_0"]},
        makes={"lists": SMEM((column_lists.size,), jnp.int32)},
    )["lists"]
    begun = call(
        "forward_0", begin_body,
        {
            "packed": at_start["packed"], "other": spread["other"], "inverse_0": at_start["inverse_0"], "lists": lists,
            **arrived,
        },
        makes={"pieces": packed_rows, "finished": all_rows, "solved": rows},
    )
    held = {1: {key: at_start[key] for key in first_blocks}}
    source = call("source", source_body, {"pieces": begun["pieces"]}, makes={"source": own_rows})["source"]
    finished, solved = begun["finished"], begun["solved"]
    to_owners = messages("row", (each, size), (each, size))
    for level in range(1, levels):
        last = level == levels - 1
        arrived = exchange("row", [solved] * len(row_routes[0]), solved)
        held.setdefault(level, {"inverses": diag_inverse, "lowers": lower_blocks})
        turned = call(
            f"turn_{level}", turn_body(level), {**held[level], "after": solved},
            makes={"turned": VMEM((1 + blocks, size, size), BF16)},
        )
        state = call(
            f"forward_{level}", forward_body(level),
            {"lists": lists, **(held[level] if last else {}), **turned, "source": source, **arrived},
            {"finished": finished},
            {"accumulated": all_rows, "answers": own_rows, **to_owners} if last else {"solved": rows},
        )
        finished, solved = state["finished"], state.get("solved")
    for level in reversed(range(1, levels - 1)):
        state = call(
            f"backward_{level}", lambda r, level=level: backward(r, level, source_of(r, level)),
            {"lists": lists, **held[level], "finished": finished, **exchanged("row", state)},
            {"accumulated": state["accumulated"], "answers": state["answers"]}, to_owners,
        )
    arrived = exchanged("row", state)
    pieces = call("gather", gather_body, {"answers": state["answers"]}, makes={"pieces": packed_rows})["pieces"]
    ended = call(
        "backward_0", last_body,
        {
            "inverse_0": at_start["inverse_0"], "finished": finished, "accumulated": state["accumulated"], **arrived,
        },
        {"pieces": pieces},
        {"kept": rows, **messages("layer", both, both)},
    )
    return call(
        "out", out_body, {"kept": ended["kept"], **exchanged("layer", ended)},
        makes={"out": jax.ShapeDtypeStruct(residual_in.shape, F32)},
        scratch={"whole": VMEM((probes, size), F32)},
    )["out"]


def solution(mesh):
    placed = (
        P(None, "row", None, "col"),
        P(None, "row", None, None),
        P(None, "row", None, None, None),
        P(),
    )
    return jax.shard_map(
        shards, mesh=mesh, in_specs=placed, out_specs=P(None, "row", None, "col"), check_vma=False
    )
```
